128 devices in a mesh: seq: 16 (over z, y_lo, core), head: 8 (over x, y_hi).
Axes of the slice: x: 4, y: 4 (y_hi: 2, y_lo: 2; y = y_hi * 2 + y_lo), z: 4, core: 2. Of those that a mesh axis runs over, the one named last changes fastest.
Arguments:
- query_in: bfloat16 [3072, 4096], P(('seq', 'head')), may hold values from -6 to 6
- key_in: bfloat16 [3072, 4096], P(('seq', 'head')), may hold values from -6 to 6
- value_in: bfloat16 [3072, 4096], P(('seq', 'head')), may hold values from -6 to 6
- grad_out: bfloat16 [3072, 4096], P(('seq', 'head')), may hold values from -6 to 6
- kernel: float32 [3, 3, 4096], P(None, None, 'head'), may hold values from 0.2 to 1
- lengths: int32 [12], replicated, may hold values from 1 to 1920, 3072 in all
Outputs:
- attended: bfloat16 [3072, 4096], P(('seq', 'head'))
- grad_query: bfloat16 [3072, 4096], P(('seq', 'head'))
- grad_key: bfloat16 [3072, 4096], P(('seq', 'head'))
- grad_value: bfloat16 [3072, 4096], P(('seq', 'head'))
The draws below stay inside these ranges and needn't reach their ends.
Inputs may be any that keep to these rules, and one draw needn't show every extreme that they name: 12 document lengths that sum to 3072; the longest is exactly 1920.
All inputs are finite; a program needn't handle non-finite values.
Results may differ from the reference program's by a relative error of at most 0.013.
The reference program's roundings to bfloat16 on the way count: a program that leaves them out, or rounds other values in their place, can miss the bound.
Values may be sent and summed in bfloat16 or wider, within the bound.
A program may use at most 128 MiB of HBM per device.

```python
import math
import jax
import jax.numpy as jnp
import numpy as np
from jax import lax

HEADS = 32
HEAD_DIM = 128
DOCS = 12
TOKENS = 3072
DOC_MOST = 1920


def base_values(key):
    drawn = jax.random.truncated_normal(key, -6.0, 6.0, (TOKENS, HEADS * HEAD_DIM))
    return drawn


def draw_query_in(key, part):
    drawn = base_values(jax.random.fold_in(key, 21))
    return drawn.astype(jnp.bfloat16)


def draw_key_in(key, part):
    drawn = base_values(jax.random.fold_in(key, 22))
    return drawn.astype(jnp.bfloat16)


def levels(key, shape, pieces, least, high):
    level = 1.0
    for dim, shards_of in pieces:
        steps = jax.random.uniform(jax.random.fold_in(jax.random.fold_in(key, 6), dim), (shards_of,), jnp.float32, least / len(pieces), high / len(pieces))
        level = level * jnp.repeat(jnp.exp(steps), shape[dim] // shards_of).reshape((-1,) + (1,) * (len(shape) - 1 - dim))
    return level


def profile(amount, total, bound, skew):
    portions = [(1 << 20) // math.isqrt(rank ** skew) + 1 for rank in range(2, amount + 1)]
    spare, counts = total - bound - (amount - 1), [1] * (amount - 1)
    while spare > 0:
        movable = [i for i in range(amount - 1) if counts[i] < bound]
        mass, left = sum([portions[i] for i in movable]), spare
        for i in movable:
            extra = min(bound - counts[i], max(1, left * portions[i] // mass), spare)
            counts[i] = counts[i] + extra
            spare = spare - extra
    return np.array([bound] + counts)


def ragged_sizes(key, amount, total, most, slope):
    if amount == 2:
        one = jax.random.randint(key, (), max(1, total - most), min(most, total - 1) + 1)
        return jnp.stack([one, total - one])
    sizes = jnp.asarray(profile(amount, total, most, slope), jnp.int32)
    pairs = (amount - 1) // 2
    source_of, sink = sizes[1:1 + 2 * pairs:2], sizes[2:2 + 2 * pairs:2]
    room = jnp.minimum(source_of - 1, most - sink)
    shifted = jax.random.randint(jax.random.fold_in(key, 1), (pairs,), 0, 1 << 20) % (room + 1)
    sizes = sizes.at[1:1 + 2 * pairs:2].set(source_of - shifted).at[2:2 + 2 * pairs:2].set(sink + shifted)
    return sizes[jax.random.permutation(jax.random.fold_in(key, 2), amount)]


def gaussian(stream_key, shape, spread, limit, pieces=(), kind=jnp.bfloat16):
    factor_of = levels(stream_key, shape, pieces, -0.22, 0.18) if pieces else 1.0
    drawn = jax.random.normal(stream_key, shape, jnp.float32) * spread * factor_of
    return jnp.minimum(jnp.maximum(drawn, -limit), limit).astype(kind)


def setup_inputs(seed: int = 0) -> dict:
    arg_keys = jax.random.split(jax.random.key(seed), 7)
    query_in = draw_query_in(jax.random.fold_in(arg_keys[6], 71), 0)
    key_in = draw_key_in(jax.random.fold_in(arg_keys[6], 71), 0)
    value_in = gaussian(arg_keys[2], (TOKENS, HEADS * HEAD_DIM), 1.0, 6.0, ((0, 128),))
    grad_out = gaussian(arg_keys[3], (TOKENS, HEADS * HEAD_DIM), 1.0, 6.0, ((0, 128),))
    kernel = jnp.clip(0.2 + 0.8 * jax.random.uniform(arg_keys[4], (3, 3, HEADS * HEAD_DIM), jnp.float32) ** levels(arg_keys[4], (3, 3, HEADS * HEAD_DIM), ((2, 8),), -0.2, 0.2), 0.2, 1.0)
    lengths = ragged_sizes(arg_keys[5], DOCS, TOKENS, DOC_MOST, 2).astype(jnp.int32)
    return dict(query_in=query_in, key_in=key_in, value_in=value_in, grad_out=grad_out, kernel=kernel, lengths=lengths)


MASKED = -1.0e30


def reference(query_in, key_in, value_in, grad_out, kernel, lengths):
    token_count = query_in.shape[0]
    positions = jnp.arange(token_count, dtype=jnp.int32)
    doc_ends = jnp.cumsum(lengths)
    segments = jnp.sum((positions[:, None] >= doc_ends[None, :]).astype(jnp.int32), axis=1)
    stacked = jnp.stack((query_in, key_in, value_in)).astype(jnp.float32)
    channels = stacked.shape[2]
    shift_one = jnp.concatenate((jnp.zeros((3, 1, channels), jnp.float32), stacked[:, :-1]), axis=1)
    shift_two = jnp.concatenate((jnp.zeros((3, 2, channels), jnp.float32), stacked[:, :-2]), axis=1)
    same_one = jnp.concatenate((jnp.zeros((1,), bool), segments[1:] == segments[:-1]))[None, :, None]
    same_two = jnp.concatenate((jnp.zeros((2,), bool), segments[2:] == segments[:-2]))[None, :, None]
    mixture = kernel[:, 0][:, None, :] * stacked + kernel[:, 1][:, None, :] * jnp.where(same_one, shift_one, 0.0)
    mixture = mixture + kernel[:, 2][:, None, :] * jnp.where(same_two, shift_two, 0.0)
    convolved = mixture.astype(jnp.bfloat16)
    allowed = (positions[None, :] <= positions[:, None]) & (segments[None, :] == segments[:, None])
    scaling = HEAD_DIM ** -0.5

    def one_head(head_index):
        def columns(array):
            return lax.dynamic_slice_in_dim(array, head_index * HEAD_DIM, HEAD_DIM, 1)

        query_head = columns(convolved[0])
        key_head = columns(convolved[1])
        value_head = columns(convolved[2])
        grad_head = columns(grad_out)
        scores = jnp.where(allowed, jnp.dot(query_head, key_head.T, preferred_element_type=jnp.float32) * scaling, MASKED)
        maxima = jnp.max(scores, axis=1)
        totals = jnp.sum(jnp.where(allowed, jnp.exp(scores - maxima[:, None]), 0.0), axis=1)
        log_norm = maxima + jnp.log(totals)
        probabilities = jnp.where(allowed, jnp.exp(scores - log_norm[:, None]), 0.0)
        head_out = jnp.dot(probabilities, value_head.astype(jnp.float32), precision=lax.Precision.HIGHEST)
        row_delta = jnp.sum(grad_head.astype(jnp.float32) * head_out, axis=1)
        dprobs = jnp.dot(grad_head, value_head.T, preferred_element_type=jnp.float32)
        dscores = (probabilities * (dprobs - row_delta[:, None])).astype(jnp.bfloat16)
        grad_qconv = jnp.dot(dscores, key_head, preferred_element_type=jnp.float32) * scaling
        grad_kconv = jnp.dot(dscores.T, query_head, preferred_element_type=jnp.float32) * scaling
        grad_vconv = jnp.dot(probabilities.astype(jnp.bfloat16).T, grad_head, preferred_element_type=jnp.float32)
        return head_out, grad_qconv, grad_kconv, grad_vconv

    results = lax.map(one_head, jnp.arange(HEADS, dtype=jnp.int32))

    def merge_heads(per_head):
        return jnp.transpose(per_head, (1, 0, 2)).reshape(token_count, HEADS * HEAD_DIM)

    head_out = merge_heads(results[0])
    conv_grads = jnp.stack((merge_heads(results[1]), merge_heads(results[2]), merge_heads(results[3])))
    next_one = jnp.concatenate((conv_grads[:, 1:], jnp.zeros((3, 1, channels), jnp.float32)), axis=1)
    next_two = jnp.concatenate((conv_grads[:, 2:], jnp.zeros((3, 2, channels), jnp.float32)), axis=1)
    after_one = jnp.concatenate((segments[1:] == segments[:-1], jnp.zeros((1,), bool)))[None, :, None]
    after_two = jnp.concatenate((segments[2:] == segments[:-2], jnp.zeros((2,), bool)))[None, :, None]
    inputs_grad = kernel[:, 0][:, None, :] * conv_grads + kernel[:, 1][:, None, :] * jnp.where(after_one, next_one, 0.0)
    inputs_grad = (inputs_grad + kernel[:, 2][:, None, :] * jnp.where(after_two, next_two, 0.0)).astype(jnp.bfloat16)
    return head_out.astype(jnp.bfloat16), inputs_grad[0], inputs_grad[1], inputs_grad[2]
```

```python
import functools

import jax
import jax.numpy as jnp
from jax import lax
from jax.experimental import pallas as pl
from jax.experimental.pallas import tpu as pltpu
from jax.sharding import Mesh
from jax.sharding import PartitionSpec as P

NAMES = ("z", "yl", "core", "x", "yh")
SIZES = (4, 2, 2, 4, 2)
D = 128
T = 3072
HEADS = 32
PIECE = 24
BLOCK = 384
PER_BLOCK = BLOCK // PIECE
OWN = 64
DOCS = 12
BQ = BLOCK
BK = 768
MASKED = -1.0e30
SCALE = D**-0.5
LOG2E = 1.4426950408889634
NT = (((1,), (1,)), ((), ()))
F32, BF16 = jnp.float32, jnp.bfloat16
MESH = pl.DeviceIdType.MESH


def dot(a, b):
    return jnp.dot(a, b, preferred_element_type=F32)


class Place:
    def __init__(self):
        self.z, self.yl, self.core, self.x, self.yh = (lax.axis_index(n) for n in NAMES)
        self.owner = lax.rem(self.x + self.z, 2) == self.yl
        self.takes = lax.rem(self.z + self.yl, 2)
        self.slot = self.z * PER_BLOCK + self.core * 8 + self.x * 2 + self.yh
        self.home = self.owner & (self.takes == self.core)

    def head_at(self, i):
        k = lax.rem(i + self.x * 8 + self.yh * 4 + self.z, HEADS)
        hx, hyh, hz = k // 8, lax.rem(k // 4, 2), lax.rem(k, 4)
        return k, dict(z=hz, yl=lax.rem(hx + hz, 2), core=self.takes, x=hx, yh=hyh)

    def token_at(self, i):
        s = lax.rem(i + self.slot, OWN)
        tz, tc, tx, tyh = s // 16, lax.rem(s // 8, 2), lax.rem(s // 2, 4), lax.rem(s, 2)
        return s, dict(z=tz, yl=lax.rem(tz + self.core, 2), core=tc, x=tx, yh=tyh)

    def sibling(self):
        return dict(z=self.z, yl=self.yl, core=1 - self.core, x=self.x, yh=self.yh)


def signal(sem, device):
    pl.semaphore_signal(sem, 1, device_id=device, device_id_type=MESH)


def remote(src, dst, send, recv, device):
    return pltpu.make_async_remote_copy(src, dst, send, recv, device_id=device, device_id_type=MESH)


def drain(ref, sem):
    pltpu.make_async_copy(ref, ref, sem).wait()


def columns(head):
    return pl.ds(pl.multiple_of(head * D, D), D)


def collect_kernel(q_ref, k_ref, v_ref, g_ref, xkv, xq, xg, xh, ssem, rsem, lsem, psem, tsem):
    me = Place()
    barrier = pltpu.get_barrier_semaphore()

    @pl.when(me.owner)
    def _():
        @pl.when(jnp.logical_not(me.home))
        def _():
            signal(barrier, me.sibling())
            _, device = me.token_at(0)
            signal(barrier, device)

        def greet(i, _):
            signal(barrier, me.token_at(i)[1])
            return 0

        lax.fori_loop(1, OWN, greet, 0)

    pl.semaphore_wait(barrier, HEADS)

    def targets(n):
        return (
            (k_ref, xkv.at[me.takes, me.slot, 0], rsem.at[0]),
            (v_ref, xkv.at[me.takes, me.slot, 1], rsem.at[0]),
            (q_ref, xq.at[me.slot], rsem.at[1]),
            (g_ref, xg.at[me.slot], rsem.at[2]),
        )[n]

    for group in ((0, 1), (2, 3)):
        def send(i, _, group=group):
            head, device = me.head_at(i)
            for n in group:
                src, dst, sem = targets(n)
                remote(src.at[:, columns(head)], dst, ssem.at[n], sem, device).start()
            return 0

        @pl.when(me.home)
        def _():
            head, _ = me.head_at(0)
            for n in group:
                src, dst, _ = targets(n)
                pltpu.make_async_copy(src.at[:, columns(head)], dst, lsem.at[n]).start()

        @pl.when(jnp.logical_not(me.home))
        def _():
            send(0, 0)

        lax.fori_loop(1, HEADS, send, 0)

    def swap():
        return remote(xkv.at[me.core], xkv.at[me.core], psem.at[0], tsem.at[0], me.sibling())

    def halo(z):
        return remote(xq.at[z * PER_BLOCK + PER_BLOCK - 1], xh.at[z], psem.at[1 + z], tsem.at[1 + z], me.sibling())

    @pl.when(me.owner)
    def _():
        @pl.when(me.home)
        def _():
            head, _ = me.head_at(0)
            for n in range(4):
                src, dst, _ = targets(n)
                pltpu.make_async_copy(src.at[:, columns(head)], dst, lsem.at[n]).wait()
            drain(xkv.at[0, pl.ds(0, OWN - 1)], rsem.at[0])

        @pl.when(jnp.logical_not(me.home))
        def _():
            drain(xkv.at[0, pl.ds(0, OWN)], rsem.at[0])

        swap().start()

        @pl.when(me.home)
        def _():
            drain(xq.at[pl.ds(0, OWN - 1)], rsem.at[1])

        @pl.when(jnp.logical_not(me.home))
        def _():
            drain(xq.at[pl.ds(0, OWN)], rsem.at[1])

        for z in range(4):
            halo(z).start()

        @pl.when(me.home)
        def _():
            drain(xg.at[pl.ds(0, OWN - 1)], rsem.at[2])

        @pl.when(jnp.logical_not(me.home))
        def _():
            drain(xg.at[pl.ds(0, OWN)], rsem.at[2])

        swap().wait()
        for z in range(4):
            halo(z).wait()

    for n, src in enumerate((k_ref, v_ref, q_ref, g_ref)):
        @pl.when(me.home)
        def _():
            drain(src.at[:, pl.ds(0, (HEADS - 1) * D)], ssem.at[n])

        @pl.when(jnp.logical_not(me.home))
        def _():
            drain(src, ssem.at[n])


def collect(q, k, v, g):
    anywhere = pl.BlockSpec(memory_space=pl.ANY)
    return pl.pallas_call(
        collect_kernel,
        out_shape=(
            jax.ShapeDtypeStruct((2, OWN, 2, PIECE, D), BF16),
            jax.ShapeDtypeStruct((OWN, PIECE, D), BF16),
            jax.ShapeDtypeStruct((OWN, PIECE, D), BF16),
            jax.ShapeDtypeStruct((4, PIECE, D), BF16),
        ),
        in_specs=[anywhere] * 4,
        out_specs=(anywhere,) * 4,
        scratch_shapes=[
            pltpu.SemaphoreType.DMA((4,)),
            pltpu.SemaphoreType.DMA((3,)),
            pltpu.SemaphoreType.DMA((4,)),
            pltpu.SemaphoreType.DMA((5,)),
            pltpu.SemaphoreType.DMA((5,)),
        ],
        compiler_params=pltpu.CompilerParams(collective_id=0, has_side_effects=True),
        name="collect",
    )(q, k, v, g)


def head_body(
    core, len_ref, kv_ref, q_ref, g_ref, halo_ref, taps_ref,
    att_ref, own_ref, other_ref, edge_ref,
    stage, hit1, hit2, qc, kc, vc, go, kt, vt, gt, sc, dq, dk, dv,
):
    starts = [jnp.int32(0)]
    for i in range(DOCS - 1):
        starts.append(starts[-1] + len_ref[i])

    def start_of(pos):
        best = jnp.zeros_like(pos)
        for s in starts[1:]:
            best = jnp.where(pos >= s, s, best)
        return best

    def base_of(c, z):
        return pl.multiple_of((z * 2 + lax.rem(z + c, 2)) * BLOCK, BLOCK)

    for a in range(3):
        stage[a, 0:8, :] = jnp.zeros((8, D), F32)

    def unpack(z, _):
        for c in range(2):
            base = base_of(c, z)
            for j in range(PER_BLOCK):
                row = base + j * PIECE
                for a in range(2):
                    stage[1 + a, pl.ds(row + 8, PIECE), :] = kv_ref[c, z * PER_BLOCK + j, a].astype(F32)
        base = base_of(core, z)
        for j in range(PER_BLOCK):
            stage[0, pl.ds(base + j * PIECE + 8, PIECE), :] = q_ref[z * PER_BLOCK + j].astype(F32)
            dq[pl.ds(base + j * PIECE, PIECE), :] = g_ref[z * PER_BLOCK + j].astype(F32)
        stage[0, pl.ds(base_of(1 - core, z) + BLOCK - PIECE + 8, PIECE), :] = halo_ref[z].astype(F32)
        return 0

    lax.fori_loop(0, 4, unpack, 0)

    def mixed(a, base, rows):
        x0 = stage[a, pl.ds(base + 8, rows), :]
        x1 = stage[a, pl.ds(base + 7, rows), :]
        x2 = stage[a, pl.ds(base + 6, rows), :]
        mix = taps_ref[3 * a : 3 * a + 1, :] * x0 + taps_ref[3 * a + 1 : 3 * a + 2, :] * (x1 * hit1[pl.ds(base, rows), :])
        return mix + taps_ref[3 * a + 2 : 3 * a + 3, :] * (x2 * hit2[pl.ds(base, rows), :])

    def keys(i, _):
        base = pl.multiple_of(i * 256, 256)
        pos = base + lax.broadcasted_iota(jnp.int32, (256, 1), 0)
        since = pos - start_of(pos)
        hit1[pl.ds(base, 256), :] = jnp.broadcast_to(jnp.where(since >= 1, 1.0, 0.0).astype(F32), (256, D))
        hit2[pl.ds(base, 256), :] = jnp.broadcast_to(jnp.where(since >= 2, 1.0, 0.0).astype(F32), (256, D))
        for a, dst, dst_t in ((1, kc, kt), (2, vc, vt)):
            mix = mixed(a, base, 256)
            dst[pl.ds(base, 256), :] = mix.astype(BF16)
            dst_t[:, pl.ds(base, 256)] = mix.T.astype(BF16)
        return 0

    lax.fori_loop(0, T // 256, keys, 0)

    def own(z, _):
        base = base_of(core, z)
        qc[pl.ds(base, BLOCK), :] = mixed(0, base, BLOCK).astype(BF16)
        g = dq[pl.ds(base, BLOCK), :]
        go[pl.ds(base, BLOCK), :] = g.astype(BF16)
        gt[:, pl.ds(base, BLOCK)] = g.T
        return 0

    lax.fori_loop(0, 4, own, 0)

    for ref in (dq, dk, dv):
        ref[...] = jnp.zeros(ref.shape, F32)
    for ref in (hit1, hit2):
        ref[T:, :] = jnp.zeros((8, D), F32)

    def queries(z, _):
        t0 = base_of(core, z)
        q = qc[pl.ds(t0, BQ), :]
        g = go[pl.ds(t0, BQ), :]
        tpos = t0 + lax.broadcasted_iota(jnp.int32, (1, BQ), 1)
        tstart = start_of(tpos)
        first = start_of(t0) // BK
        last = (t0 + BQ + BK - 1) // BK
        uio = lax.broadcasted_iota(jnp.int32, (BK, BQ), 0)

        def score(j, m):
            u0 = pl.multiple_of(j * BK, BK)
            s = lax.dot_general(kc[pl.ds(u0, BK), :], q, NT, preferred_element_type=F32)
            s = jnp.where((uio <= tpos - u0) & (uio >= tstart - u0), s, MASKED)
            sc[pl.ds(u0, BK), :] = s
            return jnp.maximum(m, jnp.max(s, axis=0, keepdims=True))

        m = lax.fori_loop(first, last, score, jnp.full((1, BQ), MASKED, F32))
        shift = m * (SCALE * LOG2E)

        def weigh(j, carry):
            total, o = carry
            u0 = pl.multiple_of(j * BK, BK)
            p = jnp.exp2(sc[pl.ds(u0, BK), :] * (SCALE * LOG2E) - shift)
            sc[pl.ds(u0, BK), :] = p
            total = total + jnp.sum(p, axis=0, keepdims=True)
            o = o + dot(vt[:, pl.ds(u0, BK)], p.astype(BF16))
            return total, o

        total, o = lax.fori_loop(first, last, weigh, (jnp.zeros((1, BQ), F32), jnp.zeros((D, BQ), F32)))
        inv = 1.0 / total
        o = o * inv
        delta = jnp.sum(gt[:, pl.ds(t0, BQ)] * o, axis=0, keepdims=True)
        stage[0, pl.ds(t0 + 8, BQ), :] = o.T

        def grads(j, acc):
            u0 = pl.multiple_of(j * BK, BK)
            p = sc[pl.ds(u0, BK), :] * inv
            dp = lax.dot_general(vc[pl.ds(u0, BK), :], g, NT, preferred_element_type=F32)
            ds = (p * (dp - delta)).astype(BF16)
            dk[pl.ds(u0, BK), :] += dot(ds, q)
            dv[pl.ds(u0, BK), :] += dot(p.astype(BF16), g)
            return acc + dot(kt[:, pl.ds(u0, BK)], ds)

        acc = lax.fori_loop(first, last, grads, jnp.zeros((D, BQ), F32))
        dq[pl.ds(t0, BQ), :] = acc.T
        return 0

    lax.fori_loop(0, 4, queries, 0)

    taps = [taps_ref[n : n + 1, :] * (SCALE if n < 6 else 1.0) for n in range(9)]

    def back(a, src, row):
        row = pl.multiple_of(row, 8)
        out = taps[3 * a] * src[pl.ds(row, PIECE), :]
        out = out + taps[3 * a + 1] * (src[pl.ds(row + 1, PIECE), :] * hit1[pl.ds(row + 1, PIECE), :])
        return out + taps[3 * a + 2] * (src[pl.ds(row + 2, PIECE), :] * hit2[pl.ds(row + 2, PIECE), :])

    def finish(z, _):
        base, across = base_of(core, z), base_of(1 - core, z)
        for j in range(PER_BLOCK):
            row, at = base + j * PIECE, z * PER_BLOCK + j
            att_ref[at] = stage[0, pl.ds(pl.multiple_of(row + 8, 8), PIECE), :].astype(BF16)
            own_ref[at, 0] = back(0, dq, row)
            own_ref[at, 1] = back(1, dk, row)
            own_ref[at, 2] = back(2, dv, row)
            row = across + j * PIECE
            other_ref[at, 0] = back(1, dk, row).astype(BF16)
            other_ref[at, 1] = back(2, dv, row).astype(BF16)
        edge_ref[z] = back(0, dq, across + BLOCK - PIECE).astype(BF16)
        return 0

    lax.fori_loop(0, 4, finish, 0)


def head_kernel(*refs):
    me = Place()

    @pl.when(me.owner)
    def _():
        head_body(me.core, *refs)


def one_head(lengths, xkv, xq, xg, xh, taps, kernel=head_kernel):
    vmem = pl.BlockSpec(memory_space=pltpu.VMEM)
    row = functools.partial(pltpu.VMEM, (T + 8, D))
    return pl.pallas_call(
        kernel,
        out_shape=(
            jax.ShapeDtypeStruct((OWN, PIECE, D), BF16),
            jax.ShapeDtypeStruct((OWN, 3, PIECE, D), F32),
            jax.ShapeDtypeStruct((OWN, 2, PIECE, D), BF16),
            jax.ShapeDtypeStruct((4, PIECE, D), BF16),
        ),
        in_specs=[pl.BlockSpec(memory_space=pltpu.SMEM)] + [vmem] * 5,
        out_specs=(vmem,) * 4,
        scratch_shapes=[
            pltpu.VMEM((3, T + 8, D), F32), row(F32), row(F32),
            pltpu.VMEM((T, D), BF16), pltpu.VMEM((T, D), BF16), pltpu.VMEM((T, D), BF16), pltpu.VMEM((T, D), BF16),
            pltpu.VMEM((D, T), BF16), pltpu.VMEM((D, T), BF16), pltpu.VMEM((D, T), F32),
            pltpu.VMEM((T, BQ), F32),
            row(F32), row(F32), row(F32),
        ],
        compiler_params=pltpu.CompilerParams(vmem_limit_bytes=48 << 20),
        name="one_head",
    )(lengths, xkv, xq, xg, xh, taps)


def spread_kernel(att, own, other, edge, out, buf, got, corner, ssem, rsem, lsem, psem, tsem):
    me = Place()
    barrier = pltpu.get_barrier_semaphore()
    @pl.when(me.home)
    def _():
        signal(barrier, me.sibling())

    @pl.when(jnp.logical_not(me.home))
    def _():
        signal(barrier, me.head_at(0)[1])

    def greet(i, _):
        signal(barrier, me.head_at(i)[1])
        return 0

    lax.fori_loop(1, HEADS, greet, 0)
    head = (me.x * 2 + me.yh) * 4 + me.z
    mine = columns(head)

    def swaps():
        return (
            remote(other, got, psem.at[0], tsem.at[0], me.sibling()),
            remote(edge, corner, psem.at[1], tsem.at[1], me.sibling()),
        )

    def send(part, i):
        s, device = me.token_at(i)
        remote(buf.at[s, part], out.at[part, :, mine], ssem, rsem, device).start()

    def keep(part, n):
        s, _ = me.token_at(0)
        return pltpu.make_async_copy(buf.at[s, part], out.at[part, :, mine], lsem.at[n])

    first, rest = pl.ds(0, 1), pl.ds(1, 3)

    def fill_att(i):
        s, _ = me.token_at(i)
        buf[s, 0] = att[s]

    def fill_rest(i):
        s, _ = me.token_at(i)
        buf[s, 1] = (own[s, 0] + jnp.where(lax.rem(s, PER_BLOCK) == PER_BLOCK - 1, corner[s // PER_BLOCK].astype(F32), 0.0)).astype(BF16)
        buf[s, 2] = (own[s, 1] + got[s, 0].astype(F32)).astype(BF16)
        buf[s, 3] = (own[s, 2] + got[s, 1].astype(F32)).astype(BF16)

    @pl.when(me.owner)
    def _():
        @pl.when(me.home)
        def _():
            pl.semaphore_wait(barrier, OWN - 1)

        @pl.when(jnp.logical_not(me.home))
        def _():
            pl.semaphore_wait(barrier, OWN + 1)

        for copy in swaps():
            copy.start()

        for part, fill, n in ((first, fill_att, 0), (rest, fill_rest, 1)):
            if n == 1:
                for copy in swaps():
                    copy.wait()
            fill(0)

            @pl.when(me.home)
            def _():
                keep(part, n).start()

            @pl.when(jnp.logical_not(me.home))
            def _():
                send(part, 0)

            def step(i, _, part=part, fill=fill):
                fill(i)
                send(part, i)
                return 0

            lax.fori_loop(1, OWN, step, 0)

        @pl.when(me.home)
        def _():
            keep(first, 0).wait()
            keep(rest, 1).wait()
            drain(buf.at[pl.ds(0, OWN - 1)], ssem)

        @pl.when(jnp.logical_not(me.home))
        def _():
            drain(buf, ssem)

    @pl.when(me.home)
    def _():
        drain(out.at[:, :, pl.ds(0, (HEADS - 1) * D)], rsem)

    @pl.when(jnp.logical_not(me.home))
    def _():
        drain(out, rsem)


def spread(att, own, other, edge):
    vmem = pl.BlockSpec(memory_space=pltpu.VMEM)
    return pl.pallas_call(
        spread_kernel,
        out_shape=jax.ShapeDtypeStruct((4, PIECE, HEADS * D), BF16),
        in_specs=[vmem] * 4,
        out_specs=pl.BlockSpec(memory_space=pl.ANY),
        scratch_shapes=[
            pltpu.VMEM((OWN, 4, PIECE, D), BF16),
            pltpu.VMEM((OWN, 2, PIECE, D), BF16),
            pltpu.VMEM((4, PIECE, D), BF16),
            pltpu.SemaphoreType.DMA,
            pltpu.SemaphoreType.DMA,
            pltpu.SemaphoreType.DMA((2,)),
            pltpu.SemaphoreType.DMA((2,)),
            pltpu.SemaphoreType.DMA((2,)),
        ],
        compiler_params=pltpu.CompilerParams(collective_id=1, has_side_effects=True),
        name="spread",
    )(att, own, other, edge)


def on_device(query_in, key_in, value_in, grad_out, kernel, lengths):
    own_head = kernel.reshape(9, 4, D)
    taps = lax.dynamic_index_in_dim(own_head, lax.axis_index("z"), 1, keepdims=False)
    xkv, xq, xg, xh = collect(query_in, key_in, value_in, grad_out)
    out = spread(*one_head(lengths, xkv, xq, xg, xh, taps))
    return tuple(out[i] for i in range(4))


def solution(mesh):
    fine = Mesh(mesh.devices.reshape(SIZES), NAMES)
    rows = P(NAMES, None)
    return jax.shard_map(
        on_device,
        mesh=fine,
        in_specs=(rows, rows, rows, rows, P(None, None, ("x", "yh")), P()),
        out_specs=(rows,) * 4,
        check_vma=False,
    )
```

```python
import functools

import jax
import jax.numpy as jnp
from jax import lax
from jax.experimental import pallas as pl
from jax.experimental.pallas import tpu as pltpu
from jax.sharding import Mesh
from jax.sharding import PartitionSpec as P

NAMES = ("z", "yl", "core", "x", "yh")
SIZES = (4, 2, 2, 4, 2)
D = 128
T = 3072
HEADS = 32
PIECE = 24
BLOCK = 384
PER_BLOCK = BLOCK // PIECE
OWN = 32
DOCS = 12
BQ = BLOCK
BK = 768
MASKED = -1.0e30
SCALE = D**-0.5
LOG2E = 1.4426950408889634
NT = (((1,), (1,)), ((), ()))
F32, BF16 = jnp.float32, jnp.bfloat16
MESH = pl.DeviceIdType.MESH


def dot(a, b):
    return jnp.dot(a, b, preferred_element_type=F32)


class Place:
    def __init__(self):
        self.z, self.yl, self.core, self.x, self.yh = (lax.axis_index(n) for n in NAMES)
        self.zbit = lax.rem(self.z, 2)
        self.head = (self.x * 2 + self.yh) * 4 + self.z
        self.slot = self.z // 2 * PER_BLOCK + self.core * 8 + self.x * 2 + self.yh
        self.side = jnp.where(self.zbit == self.yl, 0, 1)
        self.near = self.core == self.yl
        self.home = self.near & (self.side == 0)
        self.quarter = self.yl * 2 + self.core

    def owner_at(self, i, chip):
        k = lax.rem(i + self.head, HEADS)
        return k, dict(z=lax.rem(k, 4), yl=chip, core=self.yl, x=k // 8, yh=lax.rem(k // 4, 2))

    def token_at(self, i, side):
        s = lax.rem(i + self.slot, OWN)
        z = s // PER_BLOCK * 2 + lax.rem(self.yl + side, 2)
        return s, dict(z=z, yl=self.core, core=lax.rem(s // 8, 2), x=lax.rem(s // 2, 4), yh=lax.rem(s, 2))

    def other(self, yl, core):
        return dict(z=self.z, yl=yl, core=core, x=self.x, yh=self.yh)

    def sibling(self):
        return self.other(self.yl, 1 - self.core)

    def quarter_at(self, step):
        q = lax.rem(self.quarter + step + 4, 4)
        return self.other(q // 2, lax.rem(q, 2))


def signal(sem, device):
    pl.semaphore_signal(sem, 1, device_id=device, device_id_type=MESH)


def remote(src, dst, send, recv, device):
    return pltpu.make_async_remote_copy(src, dst, send, recv, device_id=device, device_id_type=MESH)


def drain(ref, sem):
    pltpu.make_async_copy(ref, ref, sem).wait()


def columns(head):
    return pl.ds(pl.multiple_of(head * D, D), D)


def settle(fewer, ref, part, sem):
    @pl.when(fewer)
    def _():
        drain(part, sem)

    @pl.when(jnp.logical_not(fewer))
    def _():
        drain(ref, sem)


def either(here, local, away):
    pl.when(here)(local)
    pl.when(jnp.logical_not(here))(away)


def most(ref):
    return ref.at[:, :, pl.ds(0, (HEADS - 1) * D)]


def collect_kernel(q_ref, k_ref, v_ref, g_ref, xkv, ykv, xqg, xh, buf, load, ssem, rsem, lsem, psem, tsem):
    me = Place()
    loads = [pltpu.make_async_copy(src, buf.at[n], load.at[n]) for n, src in enumerate((k_ref, v_ref, q_ref, g_ref))]
    for copy in loads:
        copy.start()

    barrier = pltpu.get_barrier_semaphore()
    signal(barrier, me.sibling())
    signal(barrier, me.quarter_at(-1))
    for side in range(2):
        @pl.when(jnp.logical_not(me.near & (me.side == side)))
        def _():
            signal(barrier, me.token_at(0, side)[1])

    def greet(i, _):
        for side in range(2):
            signal(barrier, me.token_at(i, side)[1])
        return 0

    lax.fori_loop(1, OWN, greet, 0)
    for copy in loads:
        copy.wait()
    either(
        me.near,
        lambda: pl.semaphore_wait(barrier, 2 * HEADS + 1),
        lambda: pl.semaphore_wait(barrier, 2 * HEADS + 2),
    )

    kv, qg = buf.at[pl.ds(0, 2)], buf.at[pl.ds(2, 2)]

    def side_at(chip):
        return jnp.where(me.zbit == chip, 0, 1)

    def send_kv(i, chip):
        head, device = me.owner_at(i, chip)
        side = side_at(chip)
        remote(kv.at[:, :, columns(head)], xkv.at[side, me.slot], ssem.at[chip], rsem.at[side], device).start()

    def send_qg(i):
        head, device = me.owner_at(i, me.zbit)
        remote(qg.at[:, :, columns(head)], xqg.at[me.slot], ssem.at[2], rsem.at[2], device).start()

    def keep_kv():
        return pltpu.make_async_copy(kv.at[:, :, columns(me.head)], xkv.at[me.side, me.slot], lsem.at[0])

    def keep_qg():
        return pltpu.make_async_copy(qg.at[:, :, columns(me.head)], xqg.at[me.slot], lsem.at[1])

    for chip in range(2):
        either(me.near & (me.yl == chip), lambda: keep_kv().start(), lambda: send_kv(0, chip))

    def all_kv(i, _):
        send_kv(i, 0)
        send_kv(i, 1)
        return 0

    lax.fori_loop(1, HEADS, all_kv, 0)
    either(me.home, lambda: keep_qg().start(), lambda: send_qg(0))

    def all_qg(i, _):
        send_qg(i)
        return 0

    lax.fori_loop(1, HEADS, all_qg, 0)

    swap = remote(xkv, ykv, psem.at[0], tsem.at[0], me.sibling())
    halos = [
        remote(xqg.at[i * PER_BLOCK + PER_BLOCK - 1, 0], xh.at[i], psem.at[1 + i], tsem.at[1 + i], me.quarter_at(1))
        for i in range(2)
    ]
    for side in range(2):
        settle(me.near & (me.side == side), xkv.at[side], xkv.at[side, pl.ds(0, OWN - 1)], rsem.at[side])
    pl.when(me.near)(lambda: keep_kv().wait())
    swap.start()
    settle(me.home, xqg, xqg.at[pl.ds(0, OWN - 1)], rsem.at[2])
    pl.when(me.home)(lambda: keep_qg().wait())
    for copy in halos:
        copy.start()
    for chip in range(2):
        settle(me.near & (me.yl == chip), kv, most(kv), ssem.at[chip])
    settle(me.home, qg, most(qg), ssem.at[2])
    swap.wait()
    for copy in halos:
        copy.wait()


def collect(q, k, v, g):
    hbm, anywhere = pl.BlockSpec(memory_space=pltpu.HBM), pl.BlockSpec(memory_space=pl.ANY)
    return pl.pallas_call(
        collect_kernel,
        out_shape=(
            pltpu.VMEM((2, OWN, 2, PIECE, D), BF16),
            pltpu.VMEM((2, OWN, 2, PIECE, D), BF16),
            pltpu.VMEM((OWN, 2, PIECE, D), BF16),
            pltpu.VMEM((2, PIECE, D), BF16),
        ),
        in_specs=[hbm] * 4,
        out_specs=(anywhere,) * 4,
        scratch_shapes=[
            pltpu.VMEM((4, PIECE, HEADS * D), BF16),
            pltpu.SemaphoreType.DMA((4,)),
            pltpu.SemaphoreType.DMA((3,)),
            pltpu.SemaphoreType.DMA((3,)),
            pltpu.SemaphoreType.DMA((2,)),
            pltpu.SemaphoreType.DMA((3,)),
            pltpu.SemaphoreType.DMA((3,)),
        ],
        compiler_params=pltpu.CompilerParams(collective_id=0, has_side_effects=True, vmem_limit_bytes=16 << 20),
        name="collect",
    )(*(pltpu.with_memory_space_constraint(x, pltpu.HBM) for x in (q, k, v, g)))


def head_body(
    yl, core, lane, len_ref, kv_ref, kv_other, qg_ref, halo_ref, all_taps,
    att_ref, dq_ref, own_ref, other_ref, edge_ref,
    stage, hit1, hit2, qc, kc, vc, go, kt, vt, gt, sc, dq, dk, dv,
):
    starts = [jnp.int32(0)]
    for i in range(DOCS - 1):
        starts.append(starts[-1] + len_ref[i])

    def start_of(pos):
        best = jnp.zeros_like(pos)
        for s in starts[1:]:
            best = jnp.where(pos >= s, s, best)
        return best

    def tap(n):
        return all_taps[n // 3, n % 3 : n % 3 + 1, pl.ds(pl.multiple_of(lane * D, D), D)]

    quarter = yl * 2 + core
    before = lax.rem(quarter + 3, 4)

    def base_of(q, i):
        return pl.multiple_of((q + 4 * i) * BLOCK, BLOCK)

    sides = [(kv, side, lax.rem(yl + side, 2) * 2 + c) for kv, c in ((kv_ref, core), (kv_other, 1 - core)) for side in range(2)]
    for a in range(3):
        stage[a, 0:8, :] = jnp.zeros((8, D), F32)

    def unpack(i, _):
        for kv, side, q in sides:
            base = base_of(q, i)
            for j in range(PER_BLOCK):
                for a in range(2):
                    stage[1 + a, pl.ds(base + j * PIECE + 8, PIECE), :] = kv[side, i * PER_BLOCK + j, a].astype(F32)
        base = base_of(quarter, i)
        for j in range(PER_BLOCK):
            stage[0, pl.ds(base + j * PIECE + 8, PIECE), :] = qg_ref[i * PER_BLOCK + j, 0].astype(F32)
            dq[pl.ds(base + j * PIECE, PIECE), :] = qg_ref[i * PER_BLOCK + j, 1].astype(F32)
        stage[0, pl.ds(base_of(before, i) + BLOCK - PIECE + 8, PIECE), :] = halo_ref[i].astype(F32)
        return 0

    lax.fori_loop(0, 2, unpack, 0)

    def mixed(a, base, rows):
        x0 = stage[a, pl.ds(base + 8, rows), :]
        x1 = stage[a, pl.ds(base + 7, rows), :]
        x2 = stage[a, pl.ds(base + 6, rows), :]
        mix = tap(3 * a) * x0 + tap(3 * a + 1) * (x1 * hit1[pl.ds(base, rows), :])
        return mix + tap(3 * a + 2) * (x2 * hit2[pl.ds(base, rows), :])

    def keys(i, _):
        base = pl.multiple_of(i * 256, 256)
        pos = base + lax.broadcasted_iota(jnp.int32, (256, 1), 0)
        since = pos - start_of(pos)
        hit1[pl.ds(base, 256), :] = jnp.broadcast_to(jnp.where(since >= 1, 1.0, 0.0).astype(F32), (256, D))
        hit2[pl.ds(base, 256), :] = jnp.broadcast_to(jnp.where(since >= 2, 1.0, 0.0).astype(F32), (256, D))
        for a, dst, dst_t in ((1, kc, kt), (2, vc, vt)):
            mix = mixed(a, base, 256)
            dst[pl.ds(base, 256), :] = mix.astype(BF16)
            dst_t[:, pl.ds(base, 256)] = mix.T.astype(BF16)
        return 0

    lax.fori_loop(0, T // 256, keys, 0)

    def own(i, _):
        base = base_of(quarter, i)
        qc[pl.ds(base, BLOCK), :] = mixed(0, base, BLOCK).astype(BF16)
        g = dq[pl.ds(base, BLOCK), :]
        go[pl.ds(base, BLOCK), :] = g.astype(BF16)
        gt[:, pl.ds(base, BLOCK)] = g.T
        return 0

    lax.fori_loop(0, 2, own, 0)

    for ref in (dq, dk, dv):
        ref[...] = jnp.zeros(ref.shape, F32)
    for ref in (hit1, hit2):
        ref[T:, :] = jnp.zeros((8, D), F32)
    for ref in (kc, vc):
        ref[T:, :] = jnp.zeros((BK, D), BF16)
    for ref in (kt, vt):
        ref[:, T:] = jnp.zeros((D, BK), BF16)

    def queries(i, _):
        t0 = base_of(quarter, i)
        q = qc[pl.ds(t0, BQ), :]
        g = go[pl.ds(t0, BQ), :]
        tpos = t0 + lax.broadcasted_iota(jnp.int32, (1, BQ), 1)
        tstart = start_of(tpos)
        from_row = start_of(t0) // D * D
        tiles = (t0 + BQ - from_row + BK - 1) // BK
        uio = lax.broadcasted_iota(jnp.int32, (BK, BQ), 0)

        def score(j, m):
            u0 = pl.multiple_of(from_row + j * BK, D)
            s = lax.dot_general(kc[pl.ds(u0, BK), :], q, NT, preferred_element_type=F32)
            s = jnp.where((uio <= tpos - u0) & (uio >= tstart - u0), s, MASKED)
            sc[pl.ds(u0, BK), :] = s
            return jnp.maximum(m, jnp.max(s, axis=0, keepdims=True))

        m = lax.fori_loop(0, tiles, score, jnp.full((1, BQ), MASKED, F32))
        shift = m * (SCALE * LOG2E)

        def weigh(j, carry):
            total, o = carry
            u0 = pl.multiple_of(from_row + j * BK, D)
            p = jnp.exp2(sc[pl.ds(u0, BK), :] * (SCALE * LOG2E) - shift)
            sc[pl.ds(u0, BK), :] = p
            total = total + jnp.sum(p, axis=0, keepdims=True)
            o = o + dot(vt[:, pl.ds(u0, BK)], p.astype(BF16))
            return total, o

        total, o = lax.fori_loop(0, tiles, weigh, (jnp.zeros((1, BQ), F32), jnp.zeros((D, BQ), F32)))
        inv = 1.0 / total
        o = o * inv
        delta = jnp.sum(gt[:, pl.ds(t0, BQ)] * o, axis=0, keepdims=True)
        stage[0, pl.ds(t0 + 8, BQ), :] = o.T

        def grads(j, acc):
            u0 = pl.multiple_of(from_row + j * BK, D)
            p = sc[pl.ds(u0, BK), :] * inv
            dp = lax.dot_general(vc[pl.ds(u0, BK), :], g, NT, preferred_element_type=F32)
            ds = (p * (dp - delta)).astype(BF16)
            dk[pl.ds(u0, BK), :] += dot(ds, q)
            dv[pl.ds(u0, BK), :] += dot(p.astype(BF16), g)
            return acc + dot(kt[:, pl.ds(u0, BK)], ds)

        acc = lax.fori_loop(0, tiles, grads, jnp.zeros((D, BQ), F32))
        dq[pl.ds(t0, BQ), :] = acc.T
        return 0

    lax.fori_loop(0, 2, queries, 0)

    taps = [tap(n) * (SCALE if n < 6 else 1.0) for n in range(9)]

    def back(a, src, row):
        row = pl.multiple_of(row, 8)
        out = taps[3 * a] * src[pl.ds(row, PIECE), :]
        out = out + taps[3 * a + 1] * (src[pl.ds(row + 1, PIECE), :] * hit1[pl.ds(row + 1, PIECE), :])
        return out + taps[3 * a + 2] * (src[pl.ds(row + 2, PIECE), :] * hit2[pl.ds(row + 2, PIECE), :])

    def finish(i, _):
        base = base_of(quarter, i)
        for j in range(PER_BLOCK):
            row, at = base + j * PIECE, i * PER_BLOCK + j
            att_ref[at] = stage[0, pl.ds(pl.multiple_of(row + 8, 8), PIECE), :].astype(BF16)
            dq_ref[at] = back(0, dq, row)
        for n, (_, side, q) in enumerate(sides):
            for j in range(PER_BLOCK):
                row, at = base_of(q, i) + j * PIECE, i * PER_BLOCK + j
                if n < 2:
                    own_ref[side, at, 0] = back(1, dk, row)
                    own_ref[side, at, 1] = back(2, dv, row)
                else:
                    other_ref[side, at, 0] = back(1, dk, row).astype(BF16)
                    other_ref[side, at, 1] = back(2, dv, row).astype(BF16)
        edge_ref[i] = back(0, dq, base_of(before, i) + BLOCK - PIECE).astype(BF16)
        return 0

    lax.fori_loop(0, 2, finish, 0)


def head_kernel(*refs):
    head_body(lax.axis_index("yl"), lax.axis_index("core"), lax.axis_index("z"), *refs)


def one_head(lengths, *arrays, kernel=head_kernel):
    vmem = pl.BlockSpec(memory_space=pltpu.VMEM)
    return pl.pallas_call(
        kernel,
        out_shape=(
            pltpu.VMEM((OWN, PIECE, D), BF16),
            pltpu.VMEM((OWN, PIECE, D), F32),
            pltpu.VMEM((2, OWN, 2, PIECE, D), F32),
            pltpu.VMEM((2, OWN, 2, PIECE, D), BF16),
            pltpu.VMEM((2, PIECE, D), BF16),
        ),
        in_specs=[pl.BlockSpec(memory_space=pltpu.SMEM)] + [vmem] * 5,
        out_specs=(vmem,) * 5,
        scratch_shapes=[
            pltpu.VMEM((3, T + 8, D), F32), pltpu.VMEM((T + 8, D), F32), pltpu.VMEM((T + 8, D), F32),
            pltpu.VMEM((T, D), BF16), pltpu.VMEM((T + BK, D), BF16), pltpu.VMEM((T + BK, D), BF16), pltpu.VMEM((T, D), BF16),
            pltpu.VMEM((D, T + BK), BF16), pltpu.VMEM((D, T + BK), BF16), pltpu.VMEM((D, T), F32),
            pltpu.VMEM((T + BK, BQ), F32),
            pltpu.VMEM((T + 8, D), F32), pltpu.VMEM((T + BK, D), F32), pltpu.VMEM((T + BK, D), F32),
        ],
        compiler_params=pltpu.CompilerParams(vmem_limit_bytes=44 << 20),
        name="one_head",
    )(lengths, *arrays)


def spread_kernel(
    att, dq, own, other, edge, out_a, out_k, buf_a, buf_k, got, corner, ssem, rsem, lsem, psem, tsem
):
    me = Place()
    barrier = pltpu.get_barrier_semaphore()
    signal(barrier, me.sibling())
    signal(barrier, me.quarter_at(1))
    for chip in range(2):
        @pl.when(jnp.logical_not(me.near & (me.yl == chip)))
        def _():
            signal(barrier, me.owner_at(0, chip)[1])

    def greet(i, _):
        for chip in range(2):
            signal(barrier, me.owner_at(i, chip)[1])
        return 0

    lax.fori_loop(1, HEADS, greet, 0)
    either(
        me.near,
        lambda: pl.semaphore_wait(barrier, 2 * OWN + 1),
        lambda: pl.semaphore_wait(barrier, 2 * OWN + 2),
    )
    swap = remote(other, got, psem.at[0], tsem.at[0], me.sibling())
    turn = remote(edge, corner, psem.at[1], tsem.at[1], me.quarter_at(-1))
    swap.start()
    turn.start()
    mine = columns(me.head)

    def fill_a(i):
        s, _ = me.token_at(i, 0)
        buf_a[s, 0] = att[s]
        last = lax.rem(s, PER_BLOCK) == PER_BLOCK - 1
        buf_a[s, 1] = (dq[s] + jnp.where(last, corner[s // PER_BLOCK].astype(F32), 0.0)).astype(BF16)

    def send_a(i):
        s, device = me.token_at(i, 0)
        remote(buf_a.at[s], out_a.at[:, :, mine], ssem.at[2], rsem.at[2], device).start()

    def keep_a():
        return pltpu.make_async_copy(buf_a.at[me.slot], out_a.at[:, :, mine], lsem.at[0])

    def fill_k(i):
        s, _ = me.token_at(i, 0)
        for side in range(2):
            buf_k[side, s] = (own[side, s] + got[side, s].astype(F32)).astype(BF16)

    def send_k(i, side):
        s, device = me.token_at(i, side)
        remote(buf_k.at[side, s], out_k.at[side, :, :, mine], ssem.at[side], rsem.at[side], device).start()

    def keep_k(side):
        return pltpu.make_async_copy(buf_k.at[side, me.slot], out_k.at[side, :, :, mine], lsem.at[1])

    turn.wait()
    fill_a(0)
    either(me.home, lambda: keep_a().start(), lambda: send_a(0))

    def all_a(i, _):
        fill_a(i)
        send_a(i)
        return 0

    lax.fori_loop(1, OWN, all_a, 0)
    swap.wait()
    fill_k(0)
    for side in range(2):
        either(me.near & (me.side == side), lambda: keep_k(side).start(), lambda: send_k(0, side))

    def all_k(i, _):
        fill_k(i)
        send_k(i, 0)
        send_k(i, 1)
        return 0

    lax.fori_loop(1, OWN, all_k, 0)
    pl.when(me.home)(lambda: keep_a().wait())
    settle(me.home, out_a, most(out_a), rsem.at[2])
    settle(me.home, buf_a, buf_a.at[pl.ds(0, OWN - 1)], ssem.at[2])
    for side in range(2):
        same = me.near & (me.side == side)
        pl.when(same)(lambda: keep_k(side).wait())
        settle(same, out_k.at[side], most(out_k.at[side]), rsem.at[side])
        settle(same, buf_k.at[side], buf_k.at[side, pl.ds(0, OWN - 1)], ssem.at[side])


def spread(*arrays):
    vmem = pl.BlockSpec(memory_space=pltpu.VMEM)
    return pl.pallas_call(
        spread_kernel,
        out_shape=(pltpu.VMEM((2, PIECE, HEADS * D), BF16), pltpu.VMEM((2, 2, PIECE, HEADS * D), BF16)),
        in_specs=[vmem] * 5,
        out_specs=(pl.BlockSpec(memory_space=pl.ANY),) * 2,
        scratch_shapes=[
            pltpu.VMEM((OWN, 2, PIECE, D), BF16),
            pltpu.VMEM((2, OWN, 2, PIECE, D), BF16),
            pltpu.VMEM((2, OWN, 2, PIECE, D), BF16),
            pltpu.VMEM((2, PIECE, D), BF16),
            pltpu.SemaphoreType.DMA((3,)),
            pltpu.SemaphoreType.DMA((3,)),
            pltpu.SemaphoreType.DMA((2,)),
            pltpu.SemaphoreType.DMA((2,)),
            pltpu.SemaphoreType.DMA((2,)),
        ],
        compiler_params=pltpu.CompilerParams(collective_id=1, has_side_effects=True, vmem_limit_bytes=32 << 20),
        name="spread",
    )(*arrays)


def on_device(query_in, key_in, value_in, grad_out, kernel, lengths):
    xkv, ykv, xqg, xh = collect(query_in, key_in, value_in, grad_out)
    plain, parts = spread(*one_head(lengths, xkv, ykv, xqg, xh, kernel))
    summed = (parts[0].astype(F32) + parts[1].astype(F32)).astype(BF16)
    return plain[0], plain[1], summed[0], summed[1]


def solution(mesh):
    fine = Mesh(mesh.devices.reshape(SIZES), NAMES)
    rows = P(NAMES, None)
    return jax.shard_map(
        on_device,
        mesh=fine,
        in_specs=(rows, rows, rows, rows, P(None, None, ("x", "yh")), P()),
        out_specs=(rows,) * 4,
        check_vma=False,
    )
```

```python
import functools

import jax
import jax.numpy as jnp
from jax import lax
from jax.experimental import pallas as pl
from jax.experimental.pallas import tpu as pltpu
from jax.sharding import Mesh
from jax.sharding import PartitionSpec as P

NAMES = ("z", "yl", "core", "x", "yh")
SIZES = (4, 2, 2, 4, 2)
D = 128
T = 3072
HEADS = 32
PIECE = 24
BLOCK = 384
PER_BLOCK = BLOCK // PIECE
OWN = 32
DOCS = 12
BQ = BLOCK
BK = 768
MASKED = -1.0e30
SCALE = D**-0.5
LOG2E = 1.4426950408889634
NT = (((1,), (1,)), ((), ()))
F32, BF16 = jnp.float32, jnp.bfloat16
MESH = pl.DeviceIdType.MESH


def dot(a, b):
    return jnp.dot(a, b, preferred_element_type=F32)


class Place:
    def __init__(self):
        self.z, self.yl, self.core, self.x, self.yh = (lax.axis_index(n) for n in NAMES)
        self.takes = lax.rem(self.z, 2)
        self.head = (self.x * 2 + self.yh) * 4 + self.z
        self.slot = self.z // 2 * PER_BLOCK + self.core * 8 + self.x * 2 + self.yh
        self.home = self.core == self.takes
        self.quarter = self.core * 2 + self.yl

    def owner_at(self, i, chip):
        k = lax.rem(i + self.head, HEADS)
        return k, dict(z=lax.rem(k, 4), yl=chip, core=self.takes, x=k // 8, yh=lax.rem(k // 4, 2))

    def token_at(self, i, side):
        s = lax.rem(i + self.slot, OWN)
        z = s // PER_BLOCK * 2 + self.core
        return s, dict(z=z, yl=lax.rem(self.yl + side, 2), core=lax.rem(s // 8, 2), x=lax.rem(s // 2, 4), yh=lax.rem(s, 2))

    def quarter_of(self, mine, side):
        return jnp.where(mine, self.core, 1 - self.core) * 2 + lax.rem(self.yl + side, 2)

    def other(self, yl, core):
        return dict(z=self.z, yl=yl, core=core, x=self.x, yh=self.yh)

    def sibling(self):
        return self.other(self.yl, 1 - self.core)

    def quarter_at(self, step):
        q = lax.rem(self.quarter + step + 4, 4)
        return self.other(lax.rem(q, 2), q // 2)


def signal(sem, device):
    pl.semaphore_signal(sem, 1, device_id=device, device_id_type=MESH)


def remote(src, dst, send, recv, device):
    return pltpu.make_async_remote_copy(src, dst, send, recv, device_id=device, device_id_type=MESH)


def drain(ref, sem):
    pltpu.make_async_copy(ref, ref, sem).wait()


def columns(head):
    return pl.ds(pl.multiple_of(head * D, D), D)


def settle(fewer, ref, part, sem):
    @pl.when(fewer)
    def _():
        drain(part, sem)

    @pl.when(jnp.logical_not(fewer))
    def _():
        drain(ref, sem)


def either(here, local, away):
    pl.when(here)(local)
    pl.when(jnp.logical_not(here))(away)


def most(ref):
    return ref.at[:, :, pl.ds(0, (HEADS - 1) * D)]


def starts_in(len_ref):
    starts = [jnp.int32(0)]
    for i in range(DOCS - 1):
        starts.append(starts[-1] + len_ref[i])
    return starts


def start_of(pos, starts):
    best = jnp.zeros_like(pos)
    for s in starts[1:]:
        best = jnp.where(pos >= s, s, best)
    return best


def base_of(quarter, i):
    return pl.multiple_of((quarter + 4 * i) * BLOCK, BLOCK)


def rows8(row):
    return pl.ds(pl.multiple_of(row, 8), PIECE)


def back(taps, hit1, hit2, src, row, token):
    out = taps[0] * src[rows8(row), :]
    out = out + taps[1] * (src[pl.ds(row + 1, PIECE), :] * hit1[pl.ds(token + 1, PIECE), :])
    return out + taps[2] * (src[pl.ds(row + 2, PIECE), :] * hit2[pl.ds(token + 2, PIECE), :])


def collect_kernel(
    q_ref, k_ref, v_ref, g_ref, all_taps, lengths,
    kc, vc, kt, vt, qc, go, gt, hit1, hit2, taps,
    xkv, ykv, xqg, xh, buf, stage, spare, size, load, ssem, rsem, lsem, psem, tsem,
):
    me = Place()
    loads = [pltpu.make_async_copy(src, buf.at[n], load.at[n]) for n, src in enumerate((k_ref, v_ref, q_ref, g_ref))]
    for copy in loads:
        copy.start()
    few = [
        pltpu.make_async_copy(all_taps.at[:, :, columns(me.z)], taps, load.at[4]),
        pltpu.make_async_copy(lengths, size, load.at[5]),
    ]
    for copy in few:
        copy.start()

    barrier = pltpu.get_barrier_semaphore()
    signal(barrier, me.sibling())
    signal(barrier, me.quarter_at(-1))
    signal(barrier, me.token_at(0, 1)[1])
    pl.when(jnp.logical_not(me.home))(lambda: signal(barrier, me.token_at(0, 0)[1]))

    def greet(i, _):
        for side in range(2):
            signal(barrier, me.token_at(i, side)[1])
        return 0

    lax.fori_loop(1, OWN, greet, 0)
    for copy in loads:
        copy.wait()
    either(
        me.home,
        lambda: pl.semaphore_wait(barrier, 2 * HEADS + 1),
        lambda: pl.semaphore_wait(barrier, 2 * HEADS + 2),
    )

    kv, qg = buf.at[pl.ds(0, 2)], buf.at[pl.ds(2, 2)]

    def side_at(chip):
        return jnp.where(me.yl == chip, 0, 1)

    def send_kv(i, chip):
        head, device = me.owner_at(i, chip)
        side = side_at(chip)
        remote(kv.at[:, :, columns(head)], xkv.at[side, me.slot], ssem.at[chip], rsem.at[side], device).start()

    def send_qg(i):
        head, device = me.owner_at(i, me.yl)
        remote(qg.at[:, :, columns(head)], xqg.at[me.slot], ssem.at[2], rsem.at[2], device).start()

    def keep_kv():
        return pltpu.make_async_copy(kv.at[:, :, columns(me.head)], xkv.at[0, me.slot], lsem.at[0])

    def keep_qg():
        return pltpu.make_async_copy(qg.at[:, :, columns(me.head)], xqg.at[me.slot], lsem.at[1])

    for chip in range(2):
        either(me.home & (me.yl == chip), lambda: keep_kv().start(), lambda: send_kv(0, chip))

    def all_kv(i, _):
        send_kv(i, 0)
        send_kv(i, 1)
        return 0

    lax.fori_loop(1, HEADS, all_kv, 0)
    either(me.home, lambda: keep_qg().start(), lambda: send_qg(0))

    def all_qg(i, _):
        send_qg(i)
        return 0

    lax.fori_loop(1, HEADS, all_qg, 0)

    swap = remote(xkv, ykv, psem.at[0], tsem.at[0], me.sibling())
    halos = [
        remote(xqg.at[i * PER_BLOCK + PER_BLOCK - 1, 0], xh.at[i], psem.at[1 + i], tsem.at[1 + i], me.quarter_at(1))
        for i in range(2)
    ]
    for copy in few:
        copy.wait()
    starts = starts_in(size)

    def hits(i, _):
        base = pl.multiple_of(i * 256, 256)
        pos = base + lax.broadcasted_iota(jnp.int32, (256, 1), 0)
        since = pos - start_of(pos, starts)
        hit1[pl.ds(base, 256), :] = jnp.broadcast_to(jnp.where(since >= 1, 1.0, 0.0).astype(F32), (256, D))
        hit2[pl.ds(base, 256), :] = jnp.broadcast_to(jnp.where(since >= 2, 1.0, 0.0).astype(F32), (256, D))
        return 0

    lax.fori_loop(0, T // 256, hits, 0)
    for ref in (hit1, hit2):
        ref[T:, :] = jnp.zeros((8, D), F32)
    for a in range(3):
        stage[a, 0:8, :] = jnp.zeros((8, D), F32)
    for ref in (kc, vc):
        ref[T:, :] = jnp.zeros((BK, D), BF16)
    for ref in (kt, vt):
        ref[:, T:] = jnp.zeros((D, BK), BF16)

    def unpack(ref, mine):
        def step(i, _):
            for side in range(2):
                base = base_of(me.quarter_of(mine, side), i)
                for j in range(PER_BLOCK):
                    for a in range(2):
                        stage[1 + a, rows8(base + j * PIECE + 8), :] = ref[side, i * PER_BLOCK + j, a].astype(F32)
            return 0

        lax.fori_loop(0, 2, step, 0)

    def mixed(a, base, rows):
        mix = taps[a, 0:1, :] * stage[a, pl.ds(base + 8, rows), :]
        mix = mix + taps[a, 1:2, :] * (stage[a, pl.ds(base + 7, rows), :] * hit1[pl.ds(base, rows), :])
        return mix + taps[a, 2:3, :] * (stage[a, pl.ds(base + 6, rows), :] * hit2[pl.ds(base, rows), :])

    settle(me.home, xkv.at[0], xkv.at[0, pl.ds(0, OWN - 1)], rsem.at[0])
    drain(xkv.at[1], rsem.at[1])
    pl.when(me.home)(lambda: keep_kv().wait())
    swap.start()
    unpack(xkv, True)
    swap.wait_recv()
    unpack(ykv, False)

    def keys(i, _):
        base = pl.multiple_of(i * 256, 256)
        for a, dst, dst_t in ((1, kc, kt), (2, vc, vt)):
            mix = mixed(a, base, 256)
            dst[pl.ds(base, 256), :] = mix.astype(BF16)
            dst_t[:, pl.ds(base, 256)] = mix.T.astype(BF16)
        return 0

    lax.fori_loop(0, T // 256, keys, 0)
    settle(me.home, xqg, xqg.at[pl.ds(0, OWN - 1)], rsem.at[2])
    pl.when(me.home)(lambda: keep_qg().wait())
    for copy in halos:
        copy.start()

    def queries(i, _):
        base = base_of(me.quarter, i)
        for j in range(PER_BLOCK):
            stage[0, rows8(base + j * PIECE + 8), :] = xqg[i * PER_BLOCK + j, 0].astype(F32)
            spare[j * PIECE : (j + 1) * PIECE, :] = xqg[i * PER_BLOCK + j, 1].astype(F32)
        g = spare[...]
        rows = pl.ds(pl.multiple_of(i * BLOCK, BLOCK), BLOCK)
        go[rows, :] = g.astype(BF16)
        gt[:, rows] = g.T
        return 0

    lax.fori_loop(0, 2, queries, 0)
    for copy in halos:
        copy.wait()
    before = lax.rem(me.quarter + 3, 4)
    for i in range(2):
        stage[0, rows8(base_of(before, i) + BLOCK - PIECE + 8), :] = xh[i].astype(F32)
    for i in range(2):
        qc[i * BLOCK : (i + 1) * BLOCK, :] = mixed(0, base_of(me.quarter, i), BLOCK).astype(BF16)
    for chip in range(2):
        settle(me.home & (me.yl == chip), kv, most(kv), ssem.at[chip])
    settle(me.home, qg, most(qg), ssem.at[2])
    swap.wait_send()


def collect(*arrays):
    vmem, hbm = pl.BlockSpec(memory_space=pltpu.VMEM), pl.BlockSpec(memory_space=pltpu.HBM)
    return pl.pallas_call(
        collect_kernel,
        out_shape=(
            pltpu.VMEM((T + BK, D), BF16), pltpu.VMEM((T + BK, D), BF16),
            pltpu.VMEM((D, T + BK), BF16), pltpu.VMEM((D, T + BK), BF16),
            pltpu.VMEM((2 * BLOCK, D), BF16), pltpu.VMEM((2 * BLOCK, D), BF16), pltpu.VMEM((D, 2 * BLOCK), F32),
            pltpu.VMEM((T + 8, D), F32), pltpu.VMEM((T + 8, D), F32),
            pltpu.VMEM((3, 3, D), F32),
        ),
        in_specs=[hbm] * 6,
        out_specs=(vmem,) * 10,
        scratch_shapes=[
            pltpu.VMEM((2, OWN, 2, PIECE, D), BF16),
            pltpu.VMEM((2, OWN, 2, PIECE, D), BF16),
            pltpu.VMEM((OWN, 2, PIECE, D), BF16),
            pltpu.VMEM((2, PIECE, D), BF16),
            pltpu.VMEM((4, PIECE, HEADS * D), BF16),
            pltpu.VMEM((3, T + 8, D), F32),
            pltpu.VMEM((BLOCK, D), F32),
            pltpu.SMEM((DOCS,), jnp.int32),
            pltpu.SemaphoreType.DMA((6,)),
            pltpu.SemaphoreType.DMA((3,)),
            pltpu.SemaphoreType.DMA((3,)),
            pltpu.SemaphoreType.DMA((2,)),
            pltpu.SemaphoreType.DMA((3,)),
            pltpu.SemaphoreType.DMA((3,)),
        ],
        compiler_params=pltpu.CompilerParams(collective_id=0, has_side_effects=True, vmem_limit_bytes=24 << 20),
        name="collect",
    )(*(pltpu.with_memory_space_constraint(x, pltpu.HBM) for x in arrays))


def head_kernel(lengths, kc, vc, kt, vt, qc, go, gt, att, dq, dk, dv, sc, size, sem):
    fetch = pltpu.make_async_copy(lengths, size, sem)
    fetch.start()
    quarter = lax.axis_index("core") * 2 + lax.axis_index("yl")
    for ref in (dk, dv):
        ref[...] = jnp.zeros(ref.shape, F32)
    for i in range(2):
        dq[i, 0:PIECE, :] = jnp.zeros((PIECE, D), F32)
        dq[i, PIECE + BLOCK :, :] = jnp.zeros((8, D), F32)
    fetch.wait()
    starts = starts_in(size)

    def queries(i, _):
        t0 = base_of(quarter, i)
        own = pl.ds(pl.multiple_of(i * BLOCK, BLOCK), BQ)
        q = qc[own, :]
        g = go[own, :]
        tpos = t0 + lax.broadcasted_iota(jnp.int32, (1, BQ), 1)
        tstart = start_of(tpos, starts)
        from_row = start_of(t0, starts) // D * D
        tiles = (t0 + BQ - from_row + BK - 1) // BK
        uio = lax.broadcasted_iota(jnp.int32, (BK, BQ), 0)

        def score(j, m):
            u0 = pl.multiple_of(from_row + j * BK, D)
            s = lax.dot_general(kc[pl.ds(u0, BK), :], q, NT, preferred_element_type=F32)
            s = jnp.where((uio <= tpos - u0) & (uio >= tstart - u0), s, MASKED)
            sc[pl.ds(u0, BK), :] = s
            return jnp.maximum(m, jnp.max(s, axis=0, keepdims=True))

        m = lax.fori_loop(0, tiles, score, jnp.full((1, BQ), MASKED, F32))
        shift = m * (SCALE * LOG2E)

        def weigh(j, carry):
            total, o = carry
            u0 = pl.multiple_of(from_row + j * BK, D)
            p = jnp.exp2(sc[pl.ds(u0, BK), :] * (SCALE * LOG2E) - shift)
            sc[pl.ds(u0, BK), :] = p
            total = total + jnp.sum(p, axis=0, keepdims=True)
            o = o + dot(vt[:, pl.ds(u0, BK)], p.astype(BF16))
            return total, o

        total, o = lax.fori_loop(0, tiles, weigh, (jnp.zeros((1, BQ), F32), jnp.zeros((D, BQ), F32)))
        inv = 1.0 / total
        o = o * inv
        delta = jnp.sum(gt[:, own] * o, axis=0, keepdims=True)
        att[own, :] = o.T

        def grads(j, acc):
            u0 = pl.multiple_of(from_row + j * BK, D)
            p = sc[pl.ds(u0, BK), :] * inv
            dp = lax.dot_general(vc[pl.ds(u0, BK), :], g, NT, preferred_element_type=F32)
            ds = (p * (dp - delta)).astype(BF16)
            dk[pl.ds(u0, BK), :] += dot(ds, q)
            dv[pl.ds(u0, BK), :] += dot(p.astype(BF16), g)
            return acc + dot(kt[:, pl.ds(u0, BK)], ds)

        acc = lax.fori_loop(0, tiles, grads, jnp.zeros((D, BQ), F32))
        dq[i, PIECE : PIECE + BLOCK, :] = acc.T
        return 0

    lax.fori_loop(0, 2, queries, 0)


def one_head(lengths, *arrays, kernel=head_kernel):
    vmem, hbm = pl.BlockSpec(memory_space=pltpu.VMEM), pl.BlockSpec(memory_space=pltpu.HBM)
    return pl.pallas_call(
        kernel,
        out_shape=(
            pltpu.VMEM((2 * BLOCK, D), F32),
            pltpu.VMEM((2, PIECE + BLOCK + 8, D), F32),
            pltpu.VMEM((T + BK, D), F32),
            pltpu.VMEM((T + BK, D), F32),
        ),
        in_specs=[hbm] + [vmem] * 7,
        out_specs=(vmem,) * 4,
        scratch_shapes=[pltpu.VMEM((T + BK, BQ), F32), pltpu.SMEM((DOCS,), jnp.int32), pltpu.SemaphoreType.DMA],
        compiler_params=pltpu.CompilerParams(vmem_limit_bytes=24 << 20),
        name="one_head",
    )(pltpu.with_memory_space_constraint(lengths, pltpu.HBM), *arrays)


def spread_kernel(
    att, dq, dk, dv, hit1, hit2, all_taps, out,
    buf_a, buf_k, other, edge, got, corner, ssem, rsem, lsem, psem, tsem,
):
    me = Place()
    out_a, out_k = out.at[2], out.at[pl.ds(0, 2)]
    barrier = pltpu.get_barrier_semaphore()
    signal(barrier, me.sibling())
    signal(barrier, me.quarter_at(1))
    for chip in range(2):
        @pl.when(jnp.logical_not(me.home & (me.yl == chip)))
        def _():
            signal(barrier, me.owner_at(0, chip)[1])

    def greet(i, _):
        for chip in range(2):
            signal(barrier, me.owner_at(i, chip)[1])
        return 0

    lax.fori_loop(1, HEADS, greet, 0)
    taps = [[all_taps[a, n : n + 1, :] * (SCALE if a < 2 else 1.0) for n in range(3)] for a in range(3)]

    def through(a, src, row, token):
        return back(taps[a], hit1, hit2, src, row, token)

    def keys_at(quarter, i, j):
        token = base_of(quarter, i) + j * PIECE
        return through(1, dk, token, token), through(2, dv, token, token)

    def rest(i, _):
        for side in range(2):
            for j in range(PER_BLOCK):
                grad_k, grad_v = keys_at(me.quarter_of(False, side), i, j)
                other[side, i * PER_BLOCK + j, 0] = grad_k.astype(BF16)
                other[side, i * PER_BLOCK + j, 1] = grad_v.astype(BF16)
        token = base_of(lax.rem(me.quarter + 3, 4), i) + BLOCK - PIECE
        after = jnp.minimum(i + jnp.where(me.quarter == 0, 1, 0), 1)
        edge[i] = through(0, dq.at[after], 0, token).astype(BF16)
        return 0

    lax.fori_loop(0, 2, rest, 0)
    either(
        me.home,
        lambda: pl.semaphore_wait(barrier, 2 * OWN + 1),
        lambda: pl.semaphore_wait(barrier, 2 * OWN + 2),
    )
    swap = remote(other, got, psem.at[0], tsem.at[0], me.sibling())
    turn = remote(edge, corner, psem.at[1], tsem.at[1], me.quarter_at(-1))
    swap.start()
    turn.start()
    mine = columns(me.head)

    def fill_a(i):
        s, _ = me.token_at(i, 0)
        block, j = s // PER_BLOCK, lax.rem(s, PER_BLOCK)
        buf_a[s, 0] = att[rows8(s * PIECE), :].astype(BF16)
        grad = through(0, dq.at[block], (j + 1) * PIECE, base_of(me.quarter, block) + j * PIECE)
        buf_a[s, 1] = (grad + jnp.where(j == PER_BLOCK - 1, corner[block].astype(F32), 0.0)).astype(BF16)

    def send_a(i):
        s, device = me.token_at(i, 0)
        remote(buf_a.at[s], out_a.at[:, :, mine], ssem.at[2], rsem.at[2], device).start()

    def keep_a():
        return pltpu.make_async_copy(buf_a.at[me.slot], out_a.at[:, :, mine], lsem.at[0])

    def fill_k(i):
        s, _ = me.token_at(i, 0)
        for side in range(2):
            grads = keys_at(me.quarter_of(True, side), s // PER_BLOCK, lax.rem(s, PER_BLOCK))
            for n, grad in enumerate(grads):
                buf_k[side, s, n] = (grad + got[side, s, n].astype(F32)).astype(BF16)

    def send_k(i, side):
        s, device = me.token_at(i, side)
        remote(buf_k.at[side, s], out_k.at[side, :, :, mine], ssem.at[side], rsem.at[side], device).start()

    def keep_k():
        return pltpu.make_async_copy(buf_k.at[0, me.slot], out_k.at[0, :, :, mine], lsem.at[1])

    turn.wait()
    fill_a(0)
    either(me.home, lambda: keep_a().start(), lambda: send_a(0))

    def all_a(i, _):
        fill_a(i)
        send_a(i)
        return 0

    lax.fori_loop(1, OWN, all_a, 0)
    swap.wait()
    fill_k(0)
    either(me.home, lambda: keep_k().start(), lambda: send_k(0, 0))
    send_k(0, 1)

    def all_k(i, _):
        fill_k(i)
        send_k(i, 0)
        send_k(i, 1)
        return 0

    lax.fori_loop(1, OWN, all_k, 0)
    for copy in (keep_a, keep_k):
        pl.when(me.home)(lambda: copy().wait())
    settle(me.home, out_a, most(out_a), rsem.at[2])
    settle(me.home, out_k.at[0], most(out_k.at[0]), rsem.at[0])
    drain(out_k.at[1], rsem.at[1])
    settle(me.home, buf_a, buf_a.at[pl.ds(0, OWN - 1)], ssem.at[2])
    settle(me.home, buf_k.at[0], buf_k.at[0, pl.ds(0, OWN - 1)], ssem.at[0])
    drain(buf_k.at[1], ssem.at[1])


def spread(*arrays):
    vmem = pl.BlockSpec(memory_space=pltpu.VMEM)
    return pl.pallas_call(
        spread_kernel,
        out_shape=pltpu.VMEM((3, 2, PIECE, HEADS * D), BF16),
        in_specs=[vmem] * 7,
        out_specs=pl.BlockSpec(memory_space=pl.ANY),
        scratch_shapes=[
            pltpu.VMEM((OWN, 2, PIECE, D), BF16),
            pltpu.VMEM((2, OWN, 2, PIECE, D), BF16),
            pltpu.VMEM((2, OWN, 2, PIECE, D), BF16),
            pltpu.VMEM((2, PIECE, D), BF16),
            pltpu.VMEM((2, OWN, 2, PIECE, D), BF16),
            pltpu.VMEM((2, PIECE, D), BF16),
            pltpu.SemaphoreType.DMA((3,)),
            pltpu.SemaphoreType.DMA((3,)),
            pltpu.SemaphoreType.DMA((2,)),
            pltpu.SemaphoreType.DMA((2,)),
            pltpu.SemaphoreType.DMA((2,)),
        ],
        compiler_params=pltpu.CompilerParams(collective_id=1, has_side_effects=True, vmem_limit_bytes=24 << 20),
        name="spread",
    )(*arrays)


def on_device(query_in, key_in, value_in, grad_out, kernel, lengths):
    *conv, hit1, hit2, taps = collect(query_in, key_in, value_in, grad_out, kernel, lengths)
    out = spread(*one_head(lengths, *conv), hit1, hit2, taps)
    summed = (out[0].astype(F32) + out[1].astype(F32)).astype(BF16)
    return out[2, 0], out[2, 1], summed[0], summed[1]


def solution(mesh):
    fine = Mesh(mesh.devices.reshape(SIZES), NAMES)
    rows = P(NAMES, None)
    return jax.shard_map(
        on_device,
        mesh=fine,
        in_specs=(rows, rows, rows, rows, P(None, None, ("x", "yh")), P()),
        out_specs=(rows,) * 4,
        check_vma=False,
    )
```

```python
import functools

import jax
import jax.numpy as jnp
from jax import lax
from jax.experimental import pallas as pl
from jax.experimental.pallas import tpu as pltpu
from jax.sharding import Mesh
from jax.sharding import PartitionSpec as P

NAMES = ("z", "yl", "core", "x", "yh")
SIZES = (4, 2, 2, 4, 2)
D = 128
T = 3072
HEADS = 32
PIECE = 24
BLOCK = 384
PER_BLOCK = BLOCK // PIECE
OWN = 32
DOCS = 12
BQ = BLOCK
BK = 768
MASKED = -1.0e30
SCALE = D**-0.5
LOG2E = 1.4426950408889634
NT = (((1,), (1,)), ((), ()))
F32, BF16 = jnp.float32, jnp.bfloat16
MESH = pl.DeviceIdType.MESH


def dot(a, b):
    return jnp.dot(a, b, preferred_element_type=F32)


class Place:
    def __init__(self):
        self.z, self.yl, self.core, self.x, self.yh = (lax.axis_index(n) for n in NAMES)
        self.takes = lax.rem(self.z, 2)
        self.head = (self.x * 2 + self.yh) * 4 + self.z
        self.slot = self.z // 2 * PER_BLOCK + self.core * 8 + self.x * 2 + self.yh
        self.home = self.core == self.takes
        self.quarter = self.core * 2 + self.yl
        self.last = (self.core == 1) & (self.x == 3) & (self.yh == 1)

    def owner_at(self, i, chip):
        k = lax.rem(i + self.head, HEADS)
        return k, dict(z=lax.rem(k, 4), yl=chip, core=self.takes, x=k // 8, yh=lax.rem(k // 4, 2))

    def token_at(self, i, side):
        s = lax.rem(i + self.slot, OWN)
        z = s // PER_BLOCK * 2 + self.core
        return s, dict(z=z, yl=lax.rem(self.yl + side, 2), core=lax.rem(s // 8, 2), x=lax.rem(s // 2, 4), yh=lax.rem(s, 2))

    def quarter_of(self, mine, side):
        return jnp.where(mine, self.core, 1 - self.core) * 2 + lax.rem(self.yl + side, 2)

    def other(self, yl, core):
        return dict(z=self.z, yl=yl, core=core, x=self.x, yh=self.yh)

    def sibling(self):
        return self.other(self.yl, 1 - self.core)

    def quarter_at(self, step):
        q = lax.rem(self.quarter + step + 4, 4)
        return self.other(lax.rem(q, 2), q // 2)

    def follower_at(self, i):
        k, device = self.owner_at(i, 0)
        q = lax.rem(self.takes * 2 + self.yl + 1, 4)
        return k, {**device, "yl": lax.rem(q, 2), "core": q // 2}

    def leader(self, i):
        q = lax.rem(self.quarter + 3, 4)
        return dict(z=q // 2 + 2 * i, yl=lax.rem(q, 2), core=1, x=3, yh=1)


def signal(sem, device):
    pl.semaphore_signal(sem, 1, device_id=device, device_id_type=MESH)


def remote(src, dst, send, recv, device):
    return pltpu.make_async_remote_copy(src, dst, send, recv, device_id=device, device_id_type=MESH)


def drain(ref, sem):
    pltpu.make_async_copy(ref, ref, sem).wait()


def columns(head):
    return pl.ds(pl.multiple_of(head * D, D), D)


def settle(fewer, ref, part, sem):
    @pl.when(fewer)
    def _():
        drain(part, sem)

    @pl.when(jnp.logical_not(fewer))
    def _():
        drain(ref, sem)


def either(here, local, away):
    pl.when(here)(local)
    pl.when(jnp.logical_not(here))(away)


def most(ref):
    return ref.at[:, :, pl.ds(0, (HEADS - 1) * D)]


def starts_in(len_ref):
    starts = [jnp.int32(0)]
    for i in range(DOCS - 1):
        starts.append(starts[-1] + len_ref[i])
    return starts


def start_of(pos, starts):
    best = jnp.zeros_like(pos)
    for s in starts[1:]:
        best = jnp.where(pos >= s, s, best)
    return best


def base_of(quarter, i):
    return pl.multiple_of((quarter + 4 * i) * BLOCK, BLOCK)


def rows8(row):
    return pl.ds(pl.multiple_of(row, 8), PIECE)


def back(taps, hit1, hit2, src, row, token):
    out = taps[0] * src[rows8(row), :]
    out = out + taps[1] * (src[pl.ds(row + 1, PIECE), :] * hit1[pl.ds(token + 1, PIECE), :])
    return out + taps[2] * (src[pl.ds(row + 2, PIECE), :] * hit2[pl.ds(token + 2, PIECE), :])


def collect_kernel(
    q_ref, k_ref, v_ref, g_ref, all_taps, lengths,
    kc, vc, kt, vt, qc, go, gt, hit1, hit2, taps,
    xkv, ykv, xqg, xh, buf, stage, spare, size, load, ssem, rsem, lsem, psem, tsem,
):
    me = Place()
    loads = [pltpu.make_async_copy(src, buf.at[n], load.at[n]) for n, src in enumerate((k_ref, v_ref, q_ref, g_ref))]
    for copy in loads:
        copy.start()
    few = [
        pltpu.make_async_copy(all_taps.at[:, :, columns(me.z)], taps, load.at[4]),
        pltpu.make_async_copy(lengths, size, load.at[5]),
    ]
    for copy in few:
        copy.start()

    barrier = pltpu.get_barrier_semaphore()
    signal(barrier, me.sibling())
    for i in range(2):
        signal(barrier, me.leader(i))
    signal(barrier, me.token_at(0, 1)[1])
    pl.when(jnp.logical_not(me.home))(lambda: signal(barrier, me.token_at(0, 0)[1]))

    def greet(i, _):
        for side in range(2):
            signal(barrier, me.token_at(i, side)[1])
        return 0

    lax.fori_loop(1, OWN, greet, 0)
    for copy in loads:
        copy.wait()
    greeted = 2 * HEADS + 1 - jnp.where(me.home, 1, 0) + jnp.where(me.last, HEADS, 0)
    pl.semaphore_wait(barrier, greeted)

    qg = buf.at[pl.ds(2, 2)]

    def side_at(chip):
        return jnp.where(me.yl == chip, 0, 1)

    def send_kv(n, i, chip):
        head, device = me.owner_at(i, chip)
        side = side_at(chip)
        remote(buf.at[n, :, columns(head)], xkv.at[n, side, me.slot], ssem.at[2 * n + chip], rsem.at[2 * n + side], device).start()

    def send_qg(i):
        head, device = me.owner_at(i, me.yl)
        remote(qg.at[:, :, columns(head)], xqg.at[me.slot], ssem.at[4], rsem.at[4], device).start()

    def keep_kv(n):
        return pltpu.make_async_copy(buf.at[n, :, columns(me.head)], xkv.at[n, 0, me.slot], lsem.at[n])

    def keep_qg():
        return pltpu.make_async_copy(qg.at[:, :, columns(me.head)], xqg.at[me.slot], lsem.at[2])

    for n in range(2):
        for chip in range(2):
            either(me.home & (me.yl == chip), lambda: keep_kv(n).start(), lambda: send_kv(n, 0, chip))

        def all_kv(i, _, n=n):
            send_kv(n, i, 0)
            send_kv(n, i, 1)
            return 0

        lax.fori_loop(1, HEADS, all_kv, 0)

    @pl.when(me.last)
    def _():
        def lead(i, _):
            head, device = me.follower_at(i)
            i = me.z // 2
            remote(buf.at[2, :, columns(head)], xh.at[i], ssem.at[5], tsem.at[i], device).start()
            return 0

        lax.fori_loop(0, HEADS, lead, 0)

    either(me.home, lambda: keep_qg().start(), lambda: send_qg(0))

    def all_qg(i, _):
        send_qg(i)
        return 0

    lax.fori_loop(1, HEADS, all_qg, 0)

    swaps = [remote(xkv.at[n], ykv.at[n], psem.at[n], tsem.at[2 + n], me.sibling()) for n in range(2)]
    for copy in few:
        copy.wait()
    starts = starts_in(size)

    def hits(i, _):
        base = pl.multiple_of(i * 256, 256)
        pos = base + lax.broadcasted_iota(jnp.int32, (256, 1), 0)
        since = pos - start_of(pos, starts)
        hit1[pl.ds(base, 256), :] = jnp.broadcast_to(jnp.where(since >= 1, 1.0, 0.0).astype(F32), (256, D))
        hit2[pl.ds(base, 256), :] = jnp.broadcast_to(jnp.where(since >= 2, 1.0, 0.0).astype(F32), (256, D))
        return 0

    lax.fori_loop(0, T // 256, hits, 0)
    for ref in (hit1, hit2):
        ref[T:, :] = jnp.zeros((8, D), F32)
    for a in range(3):
        stage[a, 0:8, :] = jnp.zeros((8, D), F32)
    for ref in (kc, vc):
        ref[T:, :] = jnp.zeros((BK, D), BF16)
    for ref in (kt, vt):
        ref[:, T:] = jnp.zeros((D, BK), BF16)

    def unpack(n, ref, mine):
        def step(i, _):
            for side in range(2):
                base = base_of(me.quarter_of(mine, side), i)
                for j in range(PER_BLOCK):
                    stage[1 + n, rows8(base + j * PIECE + 8), :] = ref[n, side, i * PER_BLOCK + j].astype(F32)
            return 0

        lax.fori_loop(0, 2, step, 0)

    def mixed(a, base, rows):
        mix = taps[a, 0:1, :] * stage[a, pl.ds(base + 8, rows), :]
        mix = mix + taps[a, 1:2, :] * (stage[a, pl.ds(base + 7, rows), :] * hit1[pl.ds(base, rows), :])
        return mix + taps[a, 2:3, :] * (stage[a, pl.ds(base + 6, rows), :] * hit2[pl.ds(base, rows), :])

    for n, (dst, dst_t) in enumerate(((kc, kt), (vc, vt))):
        settle(me.home, xkv.at[n, 0], xkv.at[n, 0, pl.ds(0, OWN - 1)], rsem.at[2 * n])
        drain(xkv.at[n, 1], rsem.at[2 * n + 1])
        pl.when(me.home)(lambda: keep_kv(n).wait())
        swaps[n].start()
        unpack(n, xkv, True)
        swaps[n].wait_recv()
        unpack(n, ykv, False)

        def keys(i, _, n=n, dst=dst, dst_t=dst_t):
            base = pl.multiple_of(i * 256, 256)
            mix = mixed(1 + n, base, 256)
            dst[pl.ds(base, 256), :] = mix.astype(BF16)
            dst_t[:, pl.ds(base, 256)] = mix.T.astype(BF16)
            return 0

        lax.fori_loop(0, T // 256, keys, 0)
    settle(me.home, xqg, xqg.at[pl.ds(0, OWN - 1)], rsem.at[4])
    pl.when(me.home)(lambda: keep_qg().wait())

    def queries(i, _):
        base = base_of(me.quarter, i)
        for j in range(PER_BLOCK):
            stage[0, rows8(base + j * PIECE + 8), :] = xqg[i * PER_BLOCK + j, 0].astype(F32)
            spare[j * PIECE : (j + 1) * PIECE, :] = xqg[i * PER_BLOCK + j, 1].astype(F32)
        g = spare[...]
        rows = pl.ds(pl.multiple_of(i * BLOCK, BLOCK), BLOCK)
        go[rows, :] = g.astype(BF16)
        gt[:, rows] = g.T
        return 0

    lax.fori_loop(0, 2, queries, 0)
    before = lax.rem(me.quarter + 3, 4)
    for i in range(2):
        drain(xh.at[i], tsem.at[i])
        stage[0, rows8(base_of(before, i) + BLOCK - PIECE + 8), :] = xh[i].astype(F32)
    for i in range(2):
        qc[i * BLOCK : (i + 1) * BLOCK, :] = mixed(0, base_of(me.quarter, i), BLOCK).astype(BF16)
    for n in range(2):
        for chip in range(2):
            fewer = buf.at[n, :, pl.ds(0, (HEADS - 1) * D)]
            settle(me.home & (me.yl == chip), buf.at[n], fewer, ssem.at[2 * n + chip])
        swaps[n].wait_send()
    settle(me.home, qg, most(qg), ssem.at[4])
    pl.when(me.last)(lambda: drain(buf.at[2], ssem.at[5]))


def collect(*arrays):
    vmem, hbm = pl.BlockSpec(memory_space=pltpu.VMEM), pl.BlockSpec(memory_space=pltpu.HBM)
    return pl.pallas_call(
        collect_kernel,
        out_shape=(
            pltpu.VMEM((T + BK, D), BF16), pltpu.VMEM((T + BK, D), BF16),
            pltpu.VMEM((D, T + BK), BF16), pltpu.VMEM((D, T + BK), BF16),
            pltpu.VMEM((2 * BLOCK, D), BF16), pltpu.VMEM((2 * BLOCK, D), BF16), pltpu.VMEM((D, 2 * BLOCK), F32),
            pltpu.VMEM((T + 8, D), F32), pltpu.VMEM((T + 8, D), F32),
            pltpu.VMEM((3, 3, D), F32),
        ),
        in_specs=[hbm] * 6,
        out_specs=(vmem,) * 10,
        scratch_shapes=[
            pltpu.VMEM((2, 2, OWN, PIECE, D), BF16),
            pltpu.VMEM((2, 2, OWN, PIECE, D), BF16),
            pltpu.VMEM((OWN, 2, PIECE, D), BF16),
            pltpu.VMEM((2, PIECE, D), BF16),
            pltpu.VMEM((4, PIECE, HEADS * D), BF16),
            pltpu.VMEM((3, T + 8, D), F32),
            pltpu.VMEM((BLOCK, D), F32),
            pltpu.SMEM((DOCS,), jnp.int32),
            pltpu.SemaphoreType.DMA((6,)),
            pltpu.SemaphoreType.DMA((6,)),
            pltpu.SemaphoreType.DMA((5,)),
            pltpu.SemaphoreType.DMA((3,)),
            pltpu.SemaphoreType.DMA((2,)),
            pltpu.SemaphoreType.DMA((4,)),
        ],
        compiler_params=pltpu.CompilerParams(collective_id=0, has_side_effects=True, vmem_limit_bytes=24 << 20),
        name="collect",
    )(*(pltpu.with_memory_space_constraint(x, pltpu.HBM) for x in arrays))


def head_kernel(lengths, kc, vc, kt, vt, qc, go, gt, att, dq, dk, dv, sc, size, sem):
    fetch = pltpu.make_async_copy(lengths, size, sem)
    fetch.start()
    quarter = lax.axis_index("core") * 2 + lax.axis_index("yl")
    for ref in (dk, dv):
        ref[...] = jnp.zeros(ref.shape, F32)
    for i in range(2):
        dq[i, 0:PIECE, :] = jnp.zeros((PIECE, D), F32)
        dq[i, PIECE + BLOCK :, :] = jnp.zeros((8, D), F32)
    fetch.wait()
    starts = starts_in(size)

    def queries(i, _):
        t0 = base_of(quarter, i)
        own = pl.ds(pl.multiple_of(i * BLOCK, BLOCK), BQ)
        q = qc[own, :]
        g = go[own, :]
        tpos = t0 + lax.broadcasted_iota(jnp.int32, (1, BQ), 1)
        tstart = start_of(tpos, starts)
        from_row = start_of(t0, starts) // D * D
        tiles = (t0 + BQ - from_row + BK - 1) // BK
        uio = lax.broadcasted_iota(jnp.int32, (BK, BQ), 0)

        def score(j, m):
            u0 = pl.multiple_of(from_row + j * BK, D)
            s = lax.dot_general(kc[pl.ds(u0, BK), :], q, NT, preferred_element_type=F32)
            s = jnp.where((uio <= tpos - u0) & (uio >= tstart - u0), s, MASKED)
            sc[pl.ds(u0, BK), :] = s
            return jnp.maximum(m, jnp.max(s, axis=0, keepdims=True))

        m = lax.fori_loop(0, tiles, score, jnp.full((1, BQ), MASKED, F32))
        shift = m * (SCALE * LOG2E)

        def weigh(j, carry):
            total, o = carry
            u0 = pl.multiple_of(from_row + j * BK, D)
            p = jnp.exp2(sc[pl.ds(u0, BK), :] * (SCALE * LOG2E) - shift)
            sc[pl.ds(u0, BK), :] = p
            total = total + jnp.sum(p, axis=0, keepdims=True)
            o = o + dot(vt[:, pl.ds(u0, BK)], p.astype(BF16))
            return total, o

        total, o = lax.fori_loop(0, tiles, weigh, (jnp.zeros((1, BQ), F32), jnp.zeros((D, BQ), F32)))
        inv = 1.0 / total
        o = o * inv
        delta = jnp.sum(gt[:, own] * o, axis=0, keepdims=True)
        att[own, :] = o.T

        def grads(j, acc):
            u0 = pl.multiple_of(from_row + j * BK, D)
            p = sc[pl.ds(u0, BK), :] * inv
            dp = lax.dot_general(vc[pl.ds(u0, BK), :], g, NT, preferred_element_type=F32)
            ds = (p * (dp - delta)).astype(BF16)
            dk[pl.ds(u0, BK), :] += dot(ds, q)
            dv[pl.ds(u0, BK), :] += dot(p.astype(BF16), g)
            return acc + dot(kt[:, pl.ds(u0, BK)], ds)

        acc = lax.fori_loop(0, tiles, grads, jnp.zeros((D, BQ), F32))
        dq[i, PIECE : PIECE + BLOCK, :] = acc.T
        return 0

    lax.fori_loop(0, 2, queries, 0)


def one_head(lengths, *arrays, kernel=head_kernel):
    vmem, hbm = pl.BlockSpec(memory_space=pltpu.VMEM), pl.BlockSpec(memory_space=pltpu.HBM)
    return pl.pallas_call(
        kernel,
        out_shape=(
            pltpu.VMEM((2 * BLOCK, D), F32),
            pltpu.VMEM((2, PIECE + BLOCK + 8, D), F32),
            pltpu.VMEM((T + BK, D), F32),
            pltpu.VMEM((T + BK, D), F32),
        ),
        in_specs=[hbm] + [vmem] * 7,
        out_specs=(vmem,) * 4,
        scratch_shapes=[pltpu.VMEM((T + BK, BQ), F32), pltpu.SMEM((DOCS,), jnp.int32), pltpu.SemaphoreType.DMA],
        compiler_params=pltpu.CompilerParams(vmem_limit_bytes=24 << 20),
        name="one_head",
    )(pltpu.with_memory_space_constraint(lengths, pltpu.HBM), *arrays)


def spread_kernel(
    att, dq, dk, dv, hit1, hit2, all_taps, out,
    buf_a, buf_k, other, edge, got, corner, ssem, rsem, lsem, psem, tsem,
):
    me = Place()
    out_a, out_k = out.at[2], out.at[pl.ds(0, 2)]
    barrier = pltpu.get_barrier_semaphore()
    signal(barrier, me.sibling())
    signal(barrier, me.quarter_at(1))
    for chip in range(2):
        @pl.when(jnp.logical_not(me.home & (me.yl == chip)))
        def _():
            signal(barrier, me.owner_at(0, chip)[1])

    def greet(i, _):
        for chip in range(2):
            signal(barrier, me.owner_at(i, chip)[1])
        return 0

    lax.fori_loop(1, HEADS, greet, 0)
    taps = [[all_taps[a, n : n + 1, :] * (SCALE if a < 2 else 1.0) for n in range(3)] for a in range(3)]

    def through(a, src, row, token):
        return back(taps[a], hit1, hit2, src, row, token)

    def keys_at(quarter, i, j):
        token = base_of(quarter, i) + j * PIECE
        return through(1, dk, token, token), through(2, dv, token, token)

    def rest(i, _):
        for side in range(2):
            for j in range(PER_BLOCK):
                grad_k, grad_v = keys_at(me.quarter_of(False, side), i, j)
                other[side, i * PER_BLOCK + j, 0] = grad_k.astype(BF16)
                other[side, i * PER_BLOCK + j, 1] = grad_v.astype(BF16)
        token = base_of(lax.rem(me.quarter + 3, 4), i) + BLOCK - PIECE
        after = jnp.minimum(i + jnp.where(me.quarter == 0, 1, 0), 1)
        edge[i] = through(0, dq.at[after], 0, token).astype(BF16)
        return 0

    lax.fori_loop(0, 2, rest, 0)
    either(
        me.home,
        lambda: pl.semaphore_wait(barrier, 2 * OWN + 1),
        lambda: pl.semaphore_wait(barrier, 2 * OWN + 2),
    )
    swap = remote(other, got, psem.at[0], tsem.at[0], me.sibling())
    turn = remote(edge, corner, psem.at[1], tsem.at[1], me.quarter_at(-1))
    swap.start()
    turn.start()
    mine = columns(me.head)

    def fill_a(i, edges):
        s, _ = me.token_at(i, 0)
        block, j = s // PER_BLOCK, lax.rem(s, PER_BLOCK)
        buf_a[s, 0] = att[rows8(s * PIECE), :].astype(BF16)
        grad = through(0, dq.at[block], (j + 1) * PIECE, base_of(me.quarter, block) + j * PIECE)
        if edges:
            grad = grad + corner[block].astype(F32)
        buf_a[s, 1] = grad.astype(BF16)

    def send_a(i):
        s, device = me.token_at(i, 0)
        remote(buf_a.at[s], out_a.at[:, :, mine], ssem.at[2], rsem.at[2], device).start()

    def keep_a():
        return pltpu.make_async_copy(buf_a.at[me.slot], out_a.at[:, :, mine], lsem.at[0])

    def fill_k(i):
        s, _ = me.token_at(i, 0)
        for side in range(2):
            grads = keys_at(me.quarter_of(True, side), s // PER_BLOCK, lax.rem(s, PER_BLOCK))
            for n, grad in enumerate(grads):
                buf_k[side, s, n] = (grad + got[side, s, n].astype(F32)).astype(BF16)

    def send_k(i, side):
        s, device = me.token_at(i, side)
        remote(buf_k.at[side, s], out_k.at[side, :, :, mine], ssem.at[side], rsem.at[side], device).start()

    def keep_k():
        return pltpu.make_async_copy(buf_k.at[0, me.slot], out_k.at[0, :, :, mine], lsem.at[1])

    def all_a(edges):
        def step(i, _):
            s, _ = me.token_at(i, 0)

            @pl.when((lax.rem(s, PER_BLOCK) == PER_BLOCK - 1) == edges)
            def _():
                fill_a(i, edges)
                either(me.home & (i == 0), lambda: keep_a().start(), lambda: send_a(i))

            return 0

        lax.fori_loop(0, OWN, step, 0)

    all_a(False)
    turn.wait()
    all_a(True)
    swap.wait()
    fill_k(0)
    either(me.home, lambda: keep_k().start(), lambda: send_k(0, 0))
    send_k(0, 1)

    def all_k(i, _):
        fill_k(i)
        send_k(i, 0)
        send_k(i, 1)
        return 0

    lax.fori_loop(1, OWN, all_k, 0)
    for copy in (keep_a, keep_k):
        pl.when(me.home)(lambda: copy().wait())
    settle(me.home, out_a, most(out_a), rsem.at[2])
    settle(me.home, out_k.at[0], most(out_k.at[0]), rsem.at[0])
    drain(out_k.at[1], rsem.at[1])
    settle(me.home, buf_a, buf_a.at[pl.ds(0, OWN - 1)], ssem.at[2])
    settle(me.home, buf_k.at[0], buf_k.at[0, pl.ds(0, OWN - 1)], ssem.at[0])
    drain(buf_k.at[1], ssem.at[1])


def spread(*arrays):
    vmem = pl.BlockSpec(memory_space=pltpu.VMEM)
    return pl.pallas_call(
        spread_kernel,
        out_shape=pltpu.VMEM((3, 2, PIECE, HEADS * D), BF16),
        in_specs=[vmem] * 7,
        out_specs=pl.BlockSpec(memory_space=pl.ANY),
        scratch_shapes=[
            pltpu.VMEM((OWN, 2, PIECE, D), BF16),
            pltpu.VMEM((2, OWN, 2, PIECE, D), BF16),
            pltpu.VMEM((2, OWN, 2, PIECE, D), BF16),
            pltpu.VMEM((2, PIECE, D), BF16),
            pltpu.VMEM((2, OWN, 2, PIECE, D), BF16),
            pltpu.VMEM((2, PIECE, D), BF16),
            pltpu.SemaphoreType.DMA((3,)),
            pltpu.SemaphoreType.DMA((3,)),
            pltpu.SemaphoreType.DMA((2,)),
            pltpu.SemaphoreType.DMA((2,)),
            pltpu.SemaphoreType.DMA((2,)),
        ],
        compiler_params=pltpu.CompilerParams(collective_id=1, has_side_effects=True, vmem_limit_bytes=24 << 20),
        name="spread",
    )(*arrays)


def on_device(query_in, key_in, value_in, grad_out, kernel, lengths):
    *conv, hit1, hit2, taps = collect(query_in, key_in, value_in, grad_out, kernel, lengths)
    out = spread(*one_head(lengths, *conv), hit1, hit2, taps)
    summed = (out[0].astype(F32) + out[1].astype(F32)).astype(BF16)
    return out[2, 0], out[2, 1], summed[0], summed[1]


def solution(mesh):
    fine = Mesh(mesh.devices.reshape(SIZES), NAMES)
    rows = P(NAMES, None)
    return jax.shard_map(
        on_device,
        mesh=fine,
        in_specs=(rows, rows, rows, rows, P(None, None, ("x", "yh")), P()),
        out_specs=(rows,) * 4,
        check_vma=False,
    )
```

```python
import functools

import jax
import jax.numpy as jnp
from jax import lax
from jax.experimental import pallas as pl
from jax.experimental.pallas import tpu as pltpu
from jax.sharding import Mesh
from jax.sharding import PartitionSpec as P

NAMES = ("z", "yl", "core", "x", "yh")
SIZES = (4, 2, 2, 4, 2)
D = 128
T = 3072
HEADS = 32
PIECE = 24
BLOCK = 384
PER_BLOCK = BLOCK // PIECE
OWN = 32
DOCS = 12
BQ = BLOCK
BK = 768
LONGEST = 1920
MASKED = -1.0e30
SCALE = D**-0.5
LOG2E = 1.4426950408889634
NT = (((1,), (1,)), ((), ()))
F32, BF16 = jnp.float32, jnp.bfloat16
MESH = pl.DeviceIdType.MESH


def dot(a, b):
    return jnp.dot(a, b, preferred_element_type=F32)


class Place:
    def __init__(self):
        self.z, self.yl, self.core, self.x, self.yh = (lax.axis_index(n) for n in NAMES)
        self.takes = lax.rem(self.z, 2)
        self.head = (self.x * 2 + self.yh) * 4 + self.z
        self.slot = self.z // 2 * PER_BLOCK + self.core * 8 + self.x * 2 + self.yh
        self.home = self.core == self.takes
        self.quarter = self.core * 2 + self.yl
        self.last = (self.core == 1) & (self.x == 3) & (self.yh == 1)

    def owner_at(self, i, chip):
        k = lax.rem(i + self.head, HEADS)
        return k, dict(z=lax.rem(k, 4), yl=chip, core=self.takes, x=k // 8, yh=lax.rem(k // 4, 2))

    def token_at(self, i, side):
        s = lax.rem(i + self.slot, OWN)
        z = s // PER_BLOCK * 2 + self.core
        return s, dict(z=z, yl=lax.rem(self.yl + side, 2), core=lax.rem(s // 8, 2), x=lax.rem(s // 2, 4), yh=lax.rem(s, 2))

    def quarter_of(self, mine, side):
        return jnp.where(mine, self.core, 1 - self.core) * 2 + lax.rem(self.yl + side, 2)

    def other(self, yl, core):
        return dict(z=self.z, yl=yl, core=core, x=self.x, yh=self.yh)

    def sibling(self):
        return self.other(self.yl, 1 - self.core)

    def quarter_at(self, step):
        q = lax.rem(self.quarter + step + 4, 4)
        return self.other(lax.rem(q, 2), q // 2)

    def follower_at(self, i):
        k, device = self.owner_at(i, 0)
        q = lax.rem(self.takes * 2 + self.yl + 1, 4)
        return k, {**device, "yl": lax.rem(q, 2), "core": q // 2}

    def leader(self, i):
        q = lax.rem(self.quarter + 3, 4)
        return dict(z=q // 2 + 2 * i, yl=lax.rem(q, 2), core=1, x=3, yh=1)


def signal(sem, device):
    pl.semaphore_signal(sem, 1, device_id=device, device_id_type=MESH)


def remote(src, dst, send, recv, device):
    return pltpu.make_async_remote_copy(src, dst, send, recv, device_id=device, device_id_type=MESH)


def drain(ref, sem):
    pltpu.make_async_copy(ref, ref, sem).wait()


def columns(head):
    return pl.ds(pl.multiple_of(head * D, D), D)


def settle(fewer, ref, part, sem):
    @pl.when(fewer)
    def _():
        drain(part, sem)

    @pl.when(jnp.logical_not(fewer))
    def _():
        drain(ref, sem)


def either(here, local, away):
    pl.when(here)(local)
    pl.when(jnp.logical_not(here))(away)


def most(ref):
    return ref.at[:, pl.ds(0, (HEADS - 1) * D)]


def starts_in(len_ref):
    starts = [jnp.int32(0)]
    for i in range(DOCS - 1):
        starts.append(starts[-1] + len_ref[i])
    return starts


def start_of(pos, starts):
    best = jnp.zeros_like(pos)
    for s in starts[1:]:
        best = jnp.where(pos >= s, s, best)
    return best


def base_of(quarter, i):
    return pl.multiple_of((quarter + 4 * i) * BLOCK, BLOCK)


def rows8(row):
    return pl.ds(pl.multiple_of(row, 8), PIECE)


def back(taps, hit1, hit2, src, row, token):
    out = taps[0] * src[rows8(row), :]
    out = out + taps[1] * (src[pl.ds(row + 1, PIECE), :] * hit1[pl.ds(token + 1, PIECE), :])
    return out + taps[2] * (src[pl.ds(row + 2, PIECE), :] * hit2[pl.ds(token + 2, PIECE), :])


KEY, VALUE, QUERY, GRAD = range(4)


def kernel_body(
    q_ref, k_ref, v_ref, g_ref, all_taps, lengths, out,
    buf, xkv, ykv, xqg, xh, stage, spare, hit1, hit2, taps, size,
    kc, vc, kt, vt, qc, go, gt, sc, peak, whole, heads_out, dq, dk, dv,
    buf_a, buf_k, other, edge, got, corner,
    load, ssem, rsem, lsem, psem, tsem,
    ssem2, rsem2, lsem2, psem2, tsem2,
):
    me = Place()
    loads = [pltpu.make_async_copy(src, buf.at[n], load.at[n]) for n, src in enumerate((k_ref, v_ref, q_ref, g_ref))]
    for copy in loads:
        copy.start()
    few = [
        pltpu.make_async_copy(all_taps.at[:, :, columns(me.z)], taps, load.at[4]),
        pltpu.make_async_copy(lengths, size, load.at[5]),
    ]
    for copy in few:
        copy.start()

    barrier = pltpu.get_barrier_semaphore()
    signal(barrier, me.sibling())
    signal(barrier, me.quarter_at(1))
    for i in range(2):
        signal(barrier, me.leader(i))
    signal(barrier, me.token_at(0, 1)[1])
    pl.when(jnp.logical_not(me.home))(lambda: signal(barrier, me.token_at(0, 0)[1]))

    def greet(i, _):
        for side in range(2):
            signal(barrier, me.token_at(i, side)[1])
        return 0

    lax.fori_loop(1, OWN, greet, 0)
    for copy in loads:
        copy.wait()
    greeted = 2 * HEADS + 2 - jnp.where(me.home, 1, 0) + jnp.where(me.last, HEADS, 0)
    pl.semaphore_wait(barrier, greeted)

    def send_kv(n, i, chip):
        head, device = me.owner_at(i, chip)
        side = jnp.where(me.yl == chip, 0, 1)
        remote(buf.at[n, :, columns(head)], xkv.at[n, side, me.slot], ssem.at[2 * n + chip], rsem.at[2 * n + side], device).start()

    def keep_kv(n):
        return pltpu.make_async_copy(buf.at[n, :, columns(me.head)], xkv.at[n, 0, me.slot], lsem.at[n])

    def send_qg(n, i):
        head, device = me.owner_at(i, me.yl)
        remote(buf.at[n, :, columns(head)], xqg.at[n - 2, me.slot], ssem.at[2 + n], rsem.at[2 + n], device).start()

    def keep_qg(n):
        return pltpu.make_async_copy(buf.at[n, :, columns(me.head)], xqg.at[n - 2, me.slot], lsem.at[n])

    for n in (KEY, QUERY, VALUE, GRAD):
        if n < 2:
            for chip in range(2):
                either(me.home & (me.yl == chip), lambda: keep_kv(n).start(), lambda: send_kv(n, 0, chip))

            def all_kv(i, _, n=n):
                send_kv(n, i, 0)
                send_kv(n, i, 1)
                return 0

            lax.fori_loop(1, HEADS, all_kv, 0)
        else:
            either(me.home, lambda: keep_qg(n).start(), lambda: send_qg(n, 0))

            def all_qg(i, _, n=n):
                send_qg(n, i)
                return 0

            lax.fori_loop(1, HEADS, all_qg, 0)
        if n == QUERY:
            @pl.when(me.last)
            def _():
                def lead(i, _):
                    head, device = me.follower_at(i)
                    block = me.z // 2
                    remote(buf.at[QUERY, :, columns(head)], xh.at[block], ssem.at[6], tsem.at[block], device).start()
                    return 0

                lax.fori_loop(0, HEADS, lead, 0)

    swaps = [remote(xkv.at[n], ykv.at[n], psem.at[n], tsem.at[2 + n], me.sibling()) for n in range(2)]
    for copy in few:
        copy.wait()
    starts = starts_in(size)

    def hits(i, _):
        base = pl.multiple_of(i * 256, 256)
        pos = base + lax.broadcasted_iota(jnp.int32, (256, 1), 0)
        since = pos - start_of(pos, starts)
        hit1[pl.ds(base, 256), :] = jnp.broadcast_to(jnp.where(since >= 1, 1.0, 0.0).astype(F32), (256, D))
        hit2[pl.ds(base, 256), :] = jnp.broadcast_to(jnp.where(since >= 2, 1.0, 0.0).astype(F32), (256, D))
        return 0

    lax.fori_loop(0, T // 256, hits, 0)
    for ref in (hit1, hit2):
        ref[T:, :] = jnp.zeros((8, D), F32)
    for a in range(3):
        stage[a, 0:8, :] = jnp.zeros((8, D), F32)
    for ref in (dk, dv):
        ref[...] = jnp.zeros(ref.shape, F32)
    for i in range(2):
        dq[i, 0:PIECE, :] = jnp.zeros((PIECE, D), F32)
        dq[i, PIECE + BLOCK :, :] = jnp.zeros((8, D), F32)

    def unpack(n, ref, mine):
        def step(i, _):
            for side in range(2):
                base = base_of(me.quarter_of(mine, side), i)
                for j in range(PER_BLOCK):
                    stage[1 + n, rows8(base + j * PIECE + 8), :] = ref[n, side, i * PER_BLOCK + j].astype(F32)
            return 0

        lax.fori_loop(0, 2, step, 0)

    def mixed(a, base, rows):
        mix = taps[a, 0:1, :] * stage[a, pl.ds(base + 8, rows), :]
        mix = mix + taps[a, 1:2, :] * (stage[a, pl.ds(base + 7, rows), :] * hit1[pl.ds(base, rows), :])
        return mix + taps[a, 2:3, :] * (stage[a, pl.ds(base + 6, rows), :] * hit2[pl.ds(base, rows), :])

    def arrive_kv(n):
        settle(me.home, xkv.at[n, 0], xkv.at[n, 0, pl.ds(0, OWN - 1)], rsem.at[2 * n])
        drain(xkv.at[n, 1], rsem.at[2 * n + 1])
        pl.when(me.home)(lambda: keep_kv(n).wait())
        swaps[n].start()

    def convolve_kv(n, dst, dst_t):
        unpack(n, xkv, True)
        swaps[n].wait_recv()
        unpack(n, ykv, False)

        def step(i, _):
            base = pl.multiple_of(i * 256, 256)
            mix = mixed(1 + n, base, 256)
            dst[pl.ds(base, 256), :] = mix.astype(BF16)
            dst_t[:, pl.ds(base, 256)] = mix.T.astype(BF16)
            return 0

        lax.fori_loop(0, T // 256, step, 0)

    def arrive_qg(n):
        settle(me.home, xqg.at[n - 2], xqg.at[n - 2, pl.ds(0, OWN - 1)], rsem.at[2 + n])
        pl.when(me.home)(lambda: keep_qg(n).wait())

    arrive_kv(KEY)
    convolve_kv(KEY, kc, kt)
    arrive_qg(QUERY)
    before = lax.rem(me.quarter + 3, 4)
    for i in range(2):
        drain(xh.at[i], tsem.at[i])
        stage[0, rows8(base_of(before, i) + BLOCK - PIECE + 8), :] = xh[i].astype(F32)

    def unpack_q(i, _):
        base = base_of(me.quarter, i)
        for j in range(PER_BLOCK):
            stage[0, rows8(base + j * PIECE + 8), :] = xqg[0, i * PER_BLOCK + j].astype(F32)
        qc[i] = mixed(0, base, BLOCK).astype(BF16)
        return 0

    lax.fori_loop(0, 2, unpack_q, 0)

    def keys_of(i):
        t0 = base_of(me.quarter, i)
        from_row = jnp.maximum(t0 - LONGEST, 0)
        return t0, from_row, (t0 + BQ - from_row + BK - 1) // BK

    def tile(from_row, j):
        return pl.multiple_of(from_row + j * BK, D)

    def scores(i):
        t0, from_row, tiles = keys_of(i)
        q = qc[i]
        tpos = t0 + lax.broadcasted_iota(jnp.int32, (1, BQ), 1)
        tstart = start_of(tpos, starts)
        uio = lax.broadcasted_iota(jnp.int32, (BK, BQ), 0)

        def score(j, m):
            u0 = tile(from_row, j)
            s = lax.dot_general(kc[pl.ds(u0, BK), :], q, NT, preferred_element_type=F32)
            s = jnp.where((uio <= tpos - u0) & (uio >= tstart - u0), s, MASKED)
            sc[i, pl.ds(u0, BK), :] = s
            return jnp.maximum(m, jnp.max(s, axis=0, keepdims=True))

        m = lax.fori_loop(0, tiles, score, jnp.full((1, BQ), MASKED, F32))
        peak[i] = m * (SCALE * LOG2E)

    def forward(i, _):
        _, from_row, tiles = keys_of(i)
        shift = peak[i]

        def weigh(j, carry):
            total, o = carry
            u0 = tile(from_row, j)
            p = jnp.exp2(sc[i, pl.ds(u0, BK), :] * (SCALE * LOG2E) - shift)
            sc[i, pl.ds(u0, BK), :] = p
            total = total + jnp.sum(p, axis=0, keepdims=True)
            o = o + dot(vt[:, pl.ds(u0, BK)], p.astype(BF16))
            return total, o

        total, o = lax.fori_loop(0, tiles, weigh, (jnp.zeros((1, BQ), F32), jnp.zeros((D, BQ), F32)))
        inv = 1.0 / total
        o = o * inv
        whole[i] = inv
        heads_out[i] = o
        spare[...] = o.T
        for j in range(PER_BLOCK):
            buf_a[0, i * PER_BLOCK + j] = spare[j * PIECE : (j + 1) * PIECE, :].astype(BF16)
        return 0

    scores(1)
    arrive_kv(VALUE)
    scores(0)
    convolve_kv(VALUE, vc, vt)
    lax.fori_loop(0, 2, forward, 0)

    mine = columns(me.head)
    out_a, out_k = out.at[2], out.at[pl.ds(0, 2)]

    def send_a(n, i):
        s, device = me.token_at(i, 0)
        remote(buf_a.at[n, s], out_a.at[n, :, mine], ssem2.at[2 + n], rsem2.at[2 + n], device).start()

    def keep_a(n):
        return pltpu.make_async_copy(buf_a.at[n, me.slot], out_a.at[n, :, mine], lsem2.at[n])

    def send_k(i, side):
        s, device = me.token_at(i, side)
        remote(buf_k.at[side, s], out_k.at[side, :, :, mine], ssem2.at[side], rsem2.at[side], device).start()

    def keep_k():
        return pltpu.make_async_copy(buf_k.at[0, me.slot], out_k.at[0, :, :, mine], lsem2.at[2])

    either(me.home, lambda: keep_a(0).start(), lambda: send_a(0, 0))

    def all_att(i, _):
        send_a(0, i)
        return 0

    lax.fori_loop(1, OWN, all_att, 0)
    arrive_qg(GRAD)

    def unpack_g(i, _):
        for j in range(PER_BLOCK):
            spare[j * PIECE : (j + 1) * PIECE, :] = xqg[1, i * PER_BLOCK + j].astype(F32)
        g = spare[...]
        go[i] = g.astype(BF16)
        gt[i] = g.T
        return 0

    lax.fori_loop(0, 2, unpack_g, 0)

    def gradients(i, _):
        _, from_row, tiles = keys_of(i)
        q, g, inv = qc[i], go[i], whole[i]
        delta = jnp.sum(gt[i] * heads_out[i], axis=0, keepdims=True)

        def grads(j, acc):
            u0 = tile(from_row, j)
            p = sc[i, pl.ds(u0, BK), :] * inv
            dp = lax.dot_general(vc[pl.ds(u0, BK), :], g, NT, preferred_element_type=F32)
            ds = (p * (dp - delta)).astype(BF16)
            dk[pl.ds(u0, BK), :] += dot(ds, q)
            dv[pl.ds(u0, BK), :] += dot(p.astype(BF16), g)
            return acc + dot(kt[:, pl.ds(u0, BK)], ds)

        acc = lax.fori_loop(0, tiles, grads, jnp.zeros((D, BQ), F32))
        dq[i, PIECE : PIECE + BLOCK, :] = acc.T
        return 0

    lax.fori_loop(0, 2, gradients, 0)
    scaled = [[taps[a, n : n + 1, :] * (SCALE if a < 2 else 1.0) for n in range(3)] for a in range(3)]

    def through(a, src, row, token):
        return back(scaled[a], hit1, hit2, src, row, token)

    def keys_at(quarter, i, j):
        token = base_of(quarter, i) + j * PIECE
        return through(1, dk, token, token), through(2, dv, token, token)

    def rest(i, _):
        for side in range(2):
            for j in range(PER_BLOCK):
                grad_k, grad_v = keys_at(me.quarter_of(False, side), i, j)
                other[side, i * PER_BLOCK + j, 0] = grad_k.astype(BF16)
                other[side, i * PER_BLOCK + j, 1] = grad_v.astype(BF16)
        token = base_of(before, i) + BLOCK - PIECE
        after = jnp.minimum(i + jnp.where(me.quarter == 0, 1, 0), 1)
        edge[i] = through(0, dq.at[after], 0, token).astype(BF16)
        return 0

    lax.fori_loop(0, 2, rest, 0)
    swap = remote(other, got, psem2.at[0], tsem2.at[0], me.sibling())
    turn = remote(edge, corner, psem2.at[1], tsem2.at[1], me.quarter_at(-1))
    swap.start()
    turn.start()

    def all_a(edges):
        def step(i, _):
            s, _ = me.token_at(i, 0)
            block, j = s // PER_BLOCK, lax.rem(s, PER_BLOCK)

            @pl.when((j == PER_BLOCK - 1) == edges)
            def _():
                grad = through(0, dq.at[block], (j + 1) * PIECE, base_of(me.quarter, block) + j * PIECE)
                if edges:
                    grad = grad + corner[block].astype(F32)
                buf_a[1, s] = grad.astype(BF16)
                either(me.home & (i == 0), lambda: keep_a(1).start(), lambda: send_a(1, i))

            return 0

        lax.fori_loop(0, OWN, step, 0)

    all_a(False)
    turn.wait()
    all_a(True)
    swap.wait()

    def fill_k(i):
        s, _ = me.token_at(i, 0)
        for side in range(2):
            grads = keys_at(me.quarter_of(True, side), s // PER_BLOCK, lax.rem(s, PER_BLOCK))
            for n, grad in enumerate(grads):
                buf_k[side, s, n] = (grad + got[side, s, n].astype(F32)).astype(BF16)

    fill_k(0)
    either(me.home, lambda: keep_k().start(), lambda: send_k(0, 0))
    send_k(0, 1)

    def all_k(i, _):
        fill_k(i)
        send_k(i, 0)
        send_k(i, 1)
        return 0

    lax.fori_loop(1, OWN, all_k, 0)

    for n in range(2):
        for chip in range(2):
            settle(me.home & (me.yl == chip), buf.at[n], most(buf.at[n]), ssem.at[2 * n + chip])
        settle(me.home, buf.at[2 + n], most(buf.at[2 + n]), ssem.at[4 + n])
        swaps[n].wait_send()
    pl.when(me.last)(lambda: drain(buf.at[QUERY], ssem.at[6]))
    for n in range(2):
        pl.when(me.home)(lambda: keep_a(n).wait())
        settle(me.home, out_a.at[n], most(out_a.at[n]), rsem2.at[2 + n])
        settle(me.home, buf_a.at[n], buf_a.at[n, pl.ds(0, OWN - 1)], ssem2.at[2 + n])
    pl.when(me.home)(lambda: keep_k().wait())
    settle(me.home, out_k.at[0], out_k.at[0, :, :, pl.ds(0, (HEADS - 1) * D)], rsem2.at[0])
    drain(out_k.at[1], rsem2.at[1])
    settle(me.home, buf_k.at[0], buf_k.at[0, pl.ds(0, OWN - 1)], ssem2.at[0])
    drain(buf_k.at[1], ssem2.at[1])


def everything(*arrays):
    hbm = pl.BlockSpec(memory_space=pltpu.HBM)
    pieces = functools.partial(pltpu.VMEM, dtype=BF16)
    dma = pltpu.SemaphoreType.DMA
    return pl.pallas_call(
        kernel_body,
        out_shape=pltpu.VMEM((3, 2, PIECE, HEADS * D), BF16),
        in_specs=[hbm] * 6,
        out_specs=pl.BlockSpec(memory_space=pl.ANY),
        scratch_shapes=[
            pieces((4, PIECE, HEADS * D)),
            pieces((2, 2, OWN, PIECE, D)), pieces((2, 2, OWN, PIECE, D)),
            pieces((2, OWN, PIECE, D)), pieces((2, PIECE, D)),
            pltpu.VMEM((3, T + 8, D), F32), pltpu.VMEM((BLOCK, D), F32),
            pltpu.VMEM((T + 8, D), F32), pltpu.VMEM((T + 8, D), F32),
            pltpu.VMEM((3, 3, D), F32), pltpu.SMEM((DOCS,), jnp.int32),
            pieces((T, D)), pieces((T, D)), pieces((D, T)), pieces((D, T)),
            pieces((2, BLOCK, D)), pieces((2, BLOCK, D)), pltpu.VMEM((2, D, BLOCK), F32),
            pltpu.VMEM((2, T, BQ), F32), pltpu.VMEM((2, 1, BQ), F32), pltpu.VMEM((2, 1, BQ), F32), pltpu.VMEM((2, D, BQ), F32),
            pltpu.VMEM((2, PIECE + BLOCK + 8, D), F32), pltpu.VMEM((T + 8, D), F32), pltpu.VMEM((T + 8, D), F32),
            pieces((2, OWN, PIECE, D)), pieces((2, OWN, 2, PIECE, D)),
            pieces((2, OWN, 2, PIECE, D)), pieces((2, PIECE, D)),
            pieces((2, OWN, 2, PIECE, D)), pieces((2, PIECE, D)),
            dma((6,)), dma((7,)), dma((6,)), dma((4,)), dma((2,)), dma((4,)),
            dma((4,)), dma((4,)), dma((3,)), dma((2,)), dma((2,)),
        ],
        compiler_params=pltpu.CompilerParams(collective_id=0, has_side_effects=True, vmem_limit_bytes=52 << 20),
        name="everything",
    )(*(pltpu.with_memory_space_constraint(x, pltpu.HBM) for x in arrays))


def on_device(query_in, key_in, value_in, grad_out, kernel, lengths):
    out = everything(query_in, key_in, value_in, grad_out, kernel, lengths)
    summed = (out[0].astype(F32) + out[1].astype(F32)).astype(BF16)
    return out[2, 0], out[2, 1], summed[0], summed[1]


def solution(mesh):
    fine = Mesh(mesh.devices.reshape(SIZES), NAMES)
    rows = P(NAMES, None)
    return jax.shard_map(
        on_device,
        mesh=fine,
        in_specs=(rows, rows, rows, rows, P(None, None, ("x", "yh")), P()),
        out_specs=(rows,) * 4,
        check_vma=False,
    )
```

```python
import functools

import jax
import jax.numpy as jnp
from jax import lax
from jax.experimental import pallas as pl
from jax.experimental.pallas import tpu as pltpu
from jax.sharding import Mesh
from jax.sharding import PartitionSpec as P

NAMES = ("z", "yl", "core", "x", "yh")
SIZES = (4, 2, 2, 4, 2)
D = 128
T = 3072
HEADS = 32
PIECE = 24
BLOCK = 384
PER_BLOCK = BLOCK // PIECE
OWN = 32
DOCS = 12
BQ = BLOCK
BK = 768
TILES = (2, 3)
LONGEST = 1920
MASKED = -1.0e30
SCALE = D**-0.5
MIX = 11
LOG2E = 1.4426950408889634
NT = (((1,), (1,)), ((), ()))
F32, BF16 = jnp.float32, jnp.bfloat16
MESH = pl.DeviceIdType.MESH


def dot(a, b):
    return jnp.dot(a, b, preferred_element_type=F32)


class Place:
    def __init__(self):
        self.z, self.yl, self.core, self.x, self.yh = (lax.axis_index(n) for n in NAMES)
        self.takes = lax.rem(self.z, 2)
        self.head = (self.x * 2 + self.yh) * 4 + self.z
        self.slot = self.z // 2 * PER_BLOCK + self.core * 8 + self.x * 2 + self.yh
        self.home = self.core == self.takes
        self.quarter = self.core * 2 + self.yl
        self.last = (self.core == 1) & (self.x == 3) & (self.yh == 1)

    def owner_at(self, i, chip):
        i = i * MIX % 32
        z, yh, x = lax.rem(self.z + i % 4, 4), lax.rem(self.yh + i // 4 % 2, 2), lax.rem(self.x + i // 8, 4)
        return (x * 2 + yh) * 4 + z, dict(z=z, yl=chip, core=self.takes, x=x, yh=yh)

    def token_at(self, i, side):
        i = i * MIX % 32
        half, core = lax.rem(self.z // 2 + i // 16, 2), lax.rem(self.core + i // 8 % 2, 2)
        x, yh = lax.rem(self.x + i // 2 % 4, 4), lax.rem(self.yh + i % 2, 2)
        device = dict(z=half * 2 + self.core, yl=lax.rem(self.yl + side, 2), core=core, x=x, yh=yh)
        return ((half * 2 + core) * 4 + x) * 2 + yh, device

    def quarter_of(self, mine, side):
        return jnp.where(mine, self.core, 1 - self.core) * 2 + lax.rem(self.yl + side, 2)

    def other(self, yl, core):
        return dict(z=self.z, yl=yl, core=core, x=self.x, yh=self.yh)

    def sibling(self):
        return self.other(self.yl, 1 - self.core)

    def quarter_at(self, step):
        q = lax.rem(self.quarter + step + 4, 4)
        return self.other(lax.rem(q, 2), q // 2)

    def follower_at(self, i):
        k, device = self.owner_at(i, 0)
        q = lax.rem(self.takes * 2 + self.yl + 1, 4)
        return k, {**device, "yl": lax.rem(q, 2), "core": q // 2}

    def leader(self, i):
        q = lax.rem(self.quarter + 3, 4)
        return dict(z=q // 2 + 2 * i, yl=lax.rem(q, 2), core=1, x=3, yh=1)


def signal(sem, device):
    pl.semaphore_signal(sem, 1, device_id=device, device_id_type=MESH)


def remote(src, dst, send, recv, device):
    return pltpu.make_async_remote_copy(src, dst, send, recv, device_id=device, device_id_type=MESH)


def drain(ref, sem):
    pltpu.make_async_copy(ref, ref, sem).wait()


def columns(head):
    return pl.ds(pl.multiple_of(head * D, D), D)


def settle(fewer, ref, part, sem):
    @pl.when(fewer)
    def _():
        drain(part, sem)

    @pl.when(jnp.logical_not(fewer))
    def _():
        drain(ref, sem)


def either(here, local, away):
    pl.when(here)(local)
    pl.when(jnp.logical_not(here))(away)


def most(ref):
    return ref.at[:, pl.ds(0, (HEADS - 1) * D)]


def each(count, step, carry):
    for j in range(count):
        carry = step(j, carry)
    return carry


def starts_in(len_ref):
    starts = [jnp.int32(0)]
    for i in range(DOCS - 1):
        starts.append(starts[-1] + len_ref[i])
    return starts


def start_of(pos, starts):
    best = jnp.zeros_like(pos)
    for s in starts[1:]:
        best = jnp.where(pos >= s, s, best)
    return best


def base_of(quarter, i):
    return pl.multiple_of((quarter + 4 * i) * BLOCK, BLOCK)


def rows8(row):
    return pl.ds(pl.multiple_of(row, 8), PIECE)


def back(taps, hit1, hit2, src, row, token):
    out = taps[0] * src[rows8(row), :]
    out = out + taps[1] * (src[pl.ds(row + 1, PIECE), :] * hit1[pl.ds(token + 1, PIECE), :])
    return out + taps[2] * (src[pl.ds(row + 2, PIECE), :] * hit2[pl.ds(token + 2, PIECE), :])


KEY, VALUE, QUERY, GRAD = range(4)


def kernel_body(
    q_ref, k_ref, v_ref, g_ref, all_taps, lengths, out,
    buf, xkv, ykv, xqg, xh, stage, spare, hit1, hit2, taps, size,
    kc, vc, kt, vt, qc, go, gt, sc, peak, whole, heads_out, dq, dk, dv,
    buf_a, buf_k, other, edge, got, corner,
    load, ssem, rsem, lsem, psem, tsem,
    ssem2, rsem2, lsem2, psem2, tsem2,
):
    me = Place()
    loads = [pltpu.make_async_copy(src, buf.at[n], load.at[n]) for n, src in enumerate((k_ref, v_ref, q_ref, g_ref))]
    for copy in loads:
        copy.start()
    few = [
        pltpu.make_async_copy(all_taps.at[:, :, columns(me.z)], taps, load.at[4]),
        pltpu.make_async_copy(lengths, size, load.at[5]),
    ]
    for copy in few:
        copy.start()

    barrier = pltpu.get_barrier_semaphore()
    signal(barrier, me.sibling())
    signal(barrier, me.quarter_at(1))
    for i in range(2):
        signal(barrier, me.leader(i))
    signal(barrier, me.token_at(0, 1)[1])
    pl.when(jnp.logical_not(me.home))(lambda: signal(barrier, me.token_at(0, 0)[1]))

    for i in range(1, OWN):
        for side in range(2):
            signal(barrier, me.token_at(i, side)[1])
    for copy in loads:
        copy.wait()
    greeted = 2 * HEADS + 2 - jnp.where(me.home, 1, 0) + jnp.where(me.last, HEADS, 0)
    pl.semaphore_wait(barrier, greeted)

    def send_kv(n, i, chip):
        head, device = me.owner_at(i, chip)
        side = jnp.where(me.yl == chip, 0, 1)
        remote(buf.at[n, :, columns(head)], xkv.at[n, side, me.slot], ssem.at[2 * n + chip], rsem.at[2 * n + side], device).start()

    def keep_kv(n):
        return pltpu.make_async_copy(buf.at[n, :, columns(me.head)], xkv.at[n, 0, me.slot], lsem.at[n])

    def send_qg(n, i):
        head, device = me.owner_at(i, me.yl)
        remote(buf.at[n, :, columns(head)], xqg.at[n - 2, me.slot], ssem.at[2 + n], rsem.at[2 + n], device).start()

    def keep_qg(n):
        return pltpu.make_async_copy(buf.at[n, :, columns(me.head)], xqg.at[n - 2, me.slot], lsem.at[n])

    for n in (KEY, QUERY, VALUE, GRAD):
        if n < 2:
            for chip in range(2):
                either(me.home & (me.yl == chip), lambda: keep_kv(n).start(), lambda: send_kv(n, 0, chip))

            for i in range(1, HEADS):
                send_kv(n, i, 0)
                send_kv(n, i, 1)
        else:
            either(me.home, lambda: keep_qg(n).start(), lambda: send_qg(n, 0))

            for i in range(1, HEADS):
                send_qg(n, i)
        if n == QUERY:
            @pl.when(me.last)
            def _():
                block = me.z // 2
                for i in range(HEADS):
                    head, device = me.follower_at(i)
                    remote(buf.at[QUERY, :, columns(head)], xh.at[block], ssem.at[6], tsem.at[block], device).start()

    swaps = [remote(xkv.at[n], ykv.at[n], psem.at[n], tsem.at[2 + n], me.sibling()) for n in range(2)]
    for copy in few:
        copy.wait()
    starts = starts_in(size)

    def hits(i, _):
        base = pl.multiple_of(i * 256, 256)
        pos = base + lax.broadcasted_iota(jnp.int32, (256, 1), 0)
        since = pos - start_of(pos, starts)
        hit1[pl.ds(base, 256), :] = jnp.broadcast_to(jnp.where(since >= 1, 1.0, 0.0).astype(F32), (256, D))
        hit2[pl.ds(base, 256), :] = jnp.broadcast_to(jnp.where(since >= 2, 1.0, 0.0).astype(F32), (256, D))
        return 0

    lax.fori_loop(0, T // 256, hits, 0)
    for ref in (hit1, hit2):
        ref[T:, :] = jnp.zeros((8, D), F32)
    for a in range(3):
        stage[a, 0:8, :] = jnp.zeros((8, D), F32)
    for ref in (dk, dv):
        ref[...] = jnp.zeros(ref.shape, F32)
    for i in range(2):
        dq[i, 0:PIECE, :] = jnp.zeros((PIECE, D), F32)
        dq[i, PIECE + BLOCK :, :] = jnp.zeros((8, D), F32)

    def unpack(n, ref, mine):
        def step(i, _):
            for side in range(2):
                base = base_of(me.quarter_of(mine, side), i)
                for j in range(PER_BLOCK):
                    stage[1 + n, rows8(base + j * PIECE + 8), :] = ref[n, side, i * PER_BLOCK + j].astype(F32)
            return 0

        lax.fori_loop(0, 2, step, 0)

    def mixed(a, base, rows):
        mix = taps[a, 0:1, :] * stage[a, pl.ds(base + 8, rows), :]
        mix = mix + taps[a, 1:2, :] * (stage[a, pl.ds(base + 7, rows), :] * hit1[pl.ds(base, rows), :])
        return mix + taps[a, 2:3, :] * (stage[a, pl.ds(base + 6, rows), :] * hit2[pl.ds(base, rows), :])

    def arrive_kv(n):
        settle(me.home, xkv.at[n, 0], xkv.at[n, 0, pl.ds(0, OWN - 1)], rsem.at[2 * n])
        drain(xkv.at[n, 1], rsem.at[2 * n + 1])
        pl.when(me.home)(lambda: keep_kv(n).wait())
        swaps[n].start()

    def convolve_kv(n, dst, dst_t):
        unpack(n, xkv, True)
        swaps[n].wait_recv()
        unpack(n, ykv, False)

        def step(i, _):
            base = pl.multiple_of(i * 256, 256)
            mix = mixed(1 + n, base, 256)
            dst[pl.ds(base, 256), :] = mix.astype(BF16)
            dst_t[:, pl.ds(base, 256)] = mix.T.astype(BF16)
            return 0

        lax.fori_loop(0, T // 256, step, 0)

    def arrive_qg(n):
        settle(me.home, xqg.at[n - 2], xqg.at[n - 2, pl.ds(0, OWN - 1)], rsem.at[2 + n])
        pl.when(me.home)(lambda: keep_qg(n).wait())

    arrive_kv(KEY)
    convolve_kv(KEY, kc, kt)
    arrive_qg(QUERY)
    before = lax.rem(me.quarter + 3, 4)
    for i in range(2):
        drain(xh.at[i], tsem.at[i])
        stage[0, rows8(base_of(before, i) + BLOCK - PIECE + 8), :] = xh[i].astype(F32)

    def unpack_q(i, _):
        base = base_of(me.quarter, i)
        for j in range(PER_BLOCK):
            stage[0, rows8(base + j * PIECE + 8), :] = xqg[0, i * PER_BLOCK + j].astype(F32)
        qc[i] = mixed(0, base, BLOCK).astype(BF16)
        return 0

    lax.fori_loop(0, 2, unpack_q, 0)

    def keys_of(i):
        t0 = base_of(me.quarter, i)
        from_row = jnp.maximum(t0 - LONGEST, 0) if i else 0
        return t0, from_row, TILES[i]

    def tile(from_row, j):
        return pl.multiple_of(from_row + j * BK, D) if not isinstance(from_row, int) else from_row + j * BK

    def scores(i):
        t0, from_row, tiles = keys_of(i)
        q = qc[i]
        tpos = t0 + lax.broadcasted_iota(jnp.int32, (1, BQ), 1)
        tstart = start_of(tpos, starts)
        uio = lax.broadcasted_iota(jnp.int32, (BK, BQ), 0)

        def score(j, m):
            u0 = tile(from_row, j)
            s = lax.dot_general(kc[pl.ds(u0, BK), :], q, NT, preferred_element_type=F32)
            s = jnp.where((uio <= tpos - u0) & (uio >= tstart - u0), s, MASKED)
            sc[i, pl.ds(u0, BK), :] = s
            return jnp.maximum(m, jnp.max(s, axis=0, keepdims=True))

        m = each(tiles, score, jnp.full((1, BQ), MASKED, F32))
        peak[i] = m * (SCALE * LOG2E)

    def forward(i, _):
        _, from_row, tiles = keys_of(i)
        shift = peak[i]

        def weigh(j, carry):
            total, o = carry
            u0 = tile(from_row, j)
            p = jnp.exp2(sc[i, pl.ds(u0, BK), :] * (SCALE * LOG2E) - shift)
            sc[i, pl.ds(u0, BK), :] = p
            total = total + jnp.sum(p, axis=0, keepdims=True)
            o = o + dot(vt[:, pl.ds(u0, BK)], p.astype(BF16))
            return total, o

        total, o = each(tiles, weigh, (jnp.zeros((1, BQ), F32), jnp.zeros((D, BQ), F32)))
        inv = 1.0 / total
        o = o * inv
        whole[i] = inv
        heads_out[i] = o
        spare[...] = o.T
        for j in range(PER_BLOCK):
            buf_a[0, i * PER_BLOCK + j] = spare[j * PIECE : (j + 1) * PIECE, :].astype(BF16)
        return 0

    scores(1)
    arrive_kv(VALUE)
    scores(0)
    convolve_kv(VALUE, vc, vt)
    for i in range(2):
        forward(i, 0)

    mine = columns(me.head)
    out_a, out_k = out.at[2], out.at[pl.ds(0, 2)]

    def send_a(n, i):
        s, device = me.token_at(i, 0)
        remote(buf_a.at[n, s], out_a.at[n, :, mine], ssem2.at[2 + n], rsem2.at[2 + n], device).start()

    def keep_a(n):
        return pltpu.make_async_copy(buf_a.at[n, me.slot], out_a.at[n, :, mine], lsem2.at[n])

    def send_k(i, side):
        s, device = me.token_at(i, side)
        remote(buf_k.at[side, s], out_k.at[side, :, :, mine], ssem2.at[side], rsem2.at[side], device).start()

    def keep_k():
        return pltpu.make_async_copy(buf_k.at[0, me.slot], out_k.at[0, :, :, mine], lsem2.at[2])

    either(me.home, lambda: keep_a(0).start(), lambda: send_a(0, 0))

    for i in range(1, OWN):
        send_a(0, i)
    arrive_qg(GRAD)

    def unpack_g(i, _):
        for j in range(PER_BLOCK):
            spare[j * PIECE : (j + 1) * PIECE, :] = xqg[1, i * PER_BLOCK + j].astype(F32)
        g = spare[...]
        go[i] = g.astype(BF16)
        gt[i] = g.T
        return 0

    lax.fori_loop(0, 2, unpack_g, 0)

    def gradients(i, _):
        _, from_row, tiles = keys_of(i)
        q, g, inv = qc[i], go[i], whole[i]
        delta = jnp.sum(gt[i] * heads_out[i], axis=0, keepdims=True)

        def grads(j, acc):
            u0 = tile(from_row, j)
            p = sc[i, pl.ds(u0, BK), :] * inv
            dp = lax.dot_general(vc[pl.ds(u0, BK), :], g, NT, preferred_element_type=F32)
            ds = (p * (dp - delta)).astype(BF16)
            dk[pl.ds(u0, BK), :] += dot(ds, q)
            dv[pl.ds(u0, BK), :] += dot(p.astype(BF16), g)
            return acc + dot(kt[:, pl.ds(u0, BK)], ds)

        acc = each(tiles, grads, jnp.zeros((D, BQ), F32))
        dq[i, PIECE : PIECE + BLOCK, :] = acc.T
        return 0

    for i in range(2):
        gradients(i, 0)
    scaled = [[taps[a, n : n + 1, :] * (SCALE if a < 2 else 1.0) for n in range(3)] for a in range(3)]

    def through(a, src, row, token):
        return back(scaled[a], hit1, hit2, src, row, token)

    def keys_at(quarter, i, j):
        token = base_of(quarter, i) + j * PIECE
        return through(1, dk, token, token), through(2, dv, token, token)

    def rest(i, _):
        for side in range(2):
            for j in range(PER_BLOCK):
                grad_k, grad_v = keys_at(me.quarter_of(False, side), i, j)
                other[side, i * PER_BLOCK + j, 0] = grad_k.astype(BF16)
                other[side, i * PER_BLOCK + j, 1] = grad_v.astype(BF16)
        token = base_of(before, i) + BLOCK - PIECE
        after = jnp.minimum(i + jnp.where(me.quarter == 0, 1, 0), 1)
        edge[i] = through(0, dq.at[after], 0, token).astype(BF16)
        return 0

    lax.fori_loop(0, 2, rest, 0)
    swap = remote(other, got, psem2.at[0], tsem2.at[0], me.sibling())
    turn = remote(edge, corner, psem2.at[1], tsem2.at[1], me.quarter_at(-1))
    swap.start()
    turn.start()

    def all_a(edges):
        for i in range(OWN):
            s, _ = me.token_at(i, 0)
            block, j = s // PER_BLOCK, lax.rem(s, PER_BLOCK)

            @pl.when((j == PER_BLOCK - 1) == edges)
            def _():
                grad = through(0, dq.at[block], (j + 1) * PIECE, base_of(me.quarter, block) + j * PIECE)
                if edges:
                    grad = grad + corner[block].astype(F32)
                buf_a[1, s] = grad.astype(BF16)
                if i:
                    send_a(1, i)
                else:
                    either(me.home, lambda: keep_a(1).start(), lambda: send_a(1, 0))

    all_a(False)
    turn.wait()
    all_a(True)
    swap.wait()

    def fill_k(i):
        s, _ = me.token_at(i, 0)
        for side in range(2):
            grads = keys_at(me.quarter_of(True, side), s // PER_BLOCK, lax.rem(s, PER_BLOCK))
            for n, grad in enumerate(grads):
                buf_k[side, s, n] = (grad + got[side, s, n].astype(F32)).astype(BF16)

    fill_k(0)
    either(me.home, lambda: keep_k().start(), lambda: send_k(0, 0))
    send_k(0, 1)

    for i in range(1, OWN):
        fill_k(i)
        send_k(i, 0)
        send_k(i, 1)

    for n in range(2):
        for chip in range(2):
            settle(me.home & (me.yl == chip), buf.at[n], most(buf.at[n]), ssem.at[2 * n + chip])
        settle(me.home, buf.at[2 + n], most(buf.at[2 + n]), ssem.at[4 + n])
        swaps[n].wait_send()
    pl.when(me.last)(lambda: drain(buf.at[QUERY], ssem.at[6]))
    for n in range(2):
        pl.when(me.home)(lambda: keep_a(n).wait())
        settle(me.home, out_a.at[n], most(out_a.at[n]), rsem2.at[2 + n])
        settle(me.home, buf_a.at[n], buf_a.at[n, pl.ds(0, OWN - 1)], ssem2.at[2 + n])
    pl.when(me.home)(lambda: keep_k().wait())
    settle(me.home, out_k.at[0], out_k.at[0, :, :, pl.ds(0, (HEADS - 1) * D)], rsem2.at[0])
    drain(out_k.at[1], rsem2.at[1])
    settle(me.home, buf_k.at[0], buf_k.at[0, pl.ds(0, OWN - 1)], ssem2.at[0])
    drain(buf_k.at[1], ssem2.at[1])


def everything(*arrays):
    hbm = pl.BlockSpec(memory_space=pltpu.HBM)
    pieces = functools.partial(pltpu.VMEM, dtype=BF16)
    dma = pltpu.SemaphoreType.DMA
    return pl.pallas_call(
        kernel_body,
        out_shape=pltpu.VMEM((3, 2, PIECE, HEADS * D), BF16),
        in_specs=[hbm] * 6,
        out_specs=pl.BlockSpec(memory_space=pl.ANY),
        scratch_shapes=[
            pieces((4, PIECE, HEADS * D)),
            pieces((2, 2, OWN, PIECE, D)), pieces((2, 2, OWN, PIECE, D)),
            pieces((2, OWN, PIECE, D)), pieces((2, PIECE, D)),
            pltpu.VMEM((3, T + 8, D), F32), pltpu.VMEM((BLOCK, D), F32),
            pltpu.VMEM((T + 8, D), F32), pltpu.VMEM((T + 8, D), F32),
            pltpu.VMEM((3, 3, D), F32), pltpu.SMEM((DOCS,), jnp.int32),
            pieces((T, D)), pieces((T, D)), pieces((D, T)), pieces((D, T)),
            pieces((2, BLOCK, D)), pieces((2, BLOCK, D)), pltpu.VMEM((2, D, BLOCK), F32),
            pltpu.VMEM((2, T, BQ), F32), pltpu.VMEM((2, 1, BQ), F32), pltpu.VMEM((2, 1, BQ), F32), pltpu.VMEM((2, D, BQ), F32),
            pltpu.VMEM((2, PIECE + BLOCK + 8, D), F32), pltpu.VMEM((T + 8, D), F32), pltpu.VMEM((T + 8, D), F32),
            pieces((2, OWN, PIECE, D)), pieces((2, OWN, 2, PIECE, D)),
            pieces((2, OWN, 2, PIECE, D)), pieces((2, PIECE, D)),
            pieces((2, OWN, 2, PIECE, D)), pieces((2, PIECE, D)),
            dma((6,)), dma((7,)), dma((6,)), dma((4,)), dma((2,)), dma((4,)),
            dma((4,)), dma((4,)), dma((3,)), dma((2,)), dma((2,)),
        ],
        compiler_params=pltpu.CompilerParams(collective_id=0, has_side_effects=True, vmem_limit_bytes=52 << 20),
        name="everything",
    )(*(pltpu.with_memory_space_constraint(x, pltpu.HBM) for x in arrays))


def on_device(query_in, key_in, value_in, grad_out, kernel, lengths):
    out = everything(query_in, key_in, value_in, grad_out, kernel, lengths)
    summed = (out[0].astype(F32) + out[1].astype(F32)).astype(BF16)
    return out[2, 0], out[2, 1], summed[0], summed[1]


def solution(mesh):
    fine = Mesh(mesh.devices.reshape(SIZES), NAMES)
    rows = P(NAMES, None)
    return jax.shard_map(
        on_device,
        mesh=fine,
        in_specs=(rows, rows, rows, rows, P(None, None, ("x", "yh")), P()),
        out_specs=(rows,) * 4,
        check_vma=False,
    )
```

```python
import functools

import jax
import jax.numpy as jnp
from jax import lax
from jax.experimental import pallas as pl
from jax.experimental.pallas import tpu as pltpu
from jax.sharding import Mesh
from jax.sharding import PartitionSpec as P

NAMES = ("z", "yl", "core", "x", "yh")
SIZES = (4, 2, 2, 4, 2)
D = 128
T = 3072
HEADS = 32
PIECE = 24
BLOCK = 384
PER_BLOCK = BLOCK // PIECE
OWN = 32
DOCS = 12
BQ = BLOCK
BK = 768
TILES = (2, 3)
LONGEST = 1920
MASKED = -1.0e30
SCALE = D**-0.5
MIX = 11
LOG2E = 1.4426950408889634
NT = (((1,), (1,)), ((), ()))
F32, BF16 = jnp.float32, jnp.bfloat16
MESH = pl.DeviceIdType.MESH


def dot(a, b):
    return jnp.dot(a, b, preferred_element_type=F32)


class Place:
    def __init__(self):
        self.z, self.yl, self.core, self.x, self.yh = (lax.axis_index(n) for n in NAMES)
        self.takes = lax.rem(self.z, 2)
        self.head = (self.x * 2 + self.yh) * 4 + self.z
        self.slot = self.z // 2 * PER_BLOCK + self.core * 8 + self.x * 2 + self.yh
        self.home = self.core == self.takes
        self.quarter = self.core * 2 + self.yl
        self.last = (self.core == 1) & (self.x == 3) & (self.yh == 1)

    def owner_at(self, i, chip):
        i = i * MIX % 32
        z, yh, x = lax.rem(self.z + i % 4, 4), lax.rem(self.yh + i // 4 % 2, 2), lax.rem(self.x + i // 8, 4)
        return (x * 2 + yh) * 4 + z, dict(z=z, yl=chip, core=self.takes, x=x, yh=yh)

    def token_at(self, i, side):
        i = i * MIX % 32
        half, core = lax.rem(self.z // 2 + i // 16, 2), lax.rem(self.core + i // 8 % 2, 2)
        x, yh = lax.rem(self.x + i // 2 % 4, 4), lax.rem(self.yh + i % 2, 2)
        device = dict(z=half * 2 + self.core, yl=lax.rem(self.yl + side, 2), core=core, x=x, yh=yh)
        return ((half * 2 + core) * 4 + x) * 2 + yh, device

    def quarter_of(self, mine, side):
        return jnp.where(mine, self.core, 1 - self.core) * 2 + lax.rem(self.yl + side, 2)

    def other(self, yl, core):
        return dict(z=self.z, yl=yl, core=core, x=self.x, yh=self.yh)

    def sibling(self):
        return self.other(self.yl, 1 - self.core)

    def quarter_at(self, step):
        q = lax.rem(self.quarter + step + 4, 4)
        return self.other(lax.rem(q, 2), q // 2)

    def follower_at(self, i):
        k, device = self.owner_at(i, 0)
        q = lax.rem(self.takes * 2 + self.yl + 1, 4)
        return k, {**device, "yl": lax.rem(q, 2), "core": q // 2}

    def leader(self, i):
        q = lax.rem(self.quarter + 3, 4)
        return dict(z=q // 2 + 2 * i, yl=lax.rem(q, 2), core=1, x=3, yh=1)


def signal(sem, device):
    pl.semaphore_signal(sem, 1, device_id=device, device_id_type=MESH)


def remote(src, dst, send, recv, device):
    return pltpu.make_async_remote_copy(src, dst, send, recv, device_id=device, device_id_type=MESH)


def drain(ref, sem):
    pltpu.make_async_copy(ref, ref, sem).wait()


def columns(head):
    return pl.ds(pl.multiple_of(head * D, D), D)


def settle(fewer, ref, part, sem):
    @pl.when(fewer)
    def _():
        drain(part, sem)

    @pl.when(jnp.logical_not(fewer))
    def _():
        drain(ref, sem)


def either(here, local, away):
    pl.when(here)(local)
    pl.when(jnp.logical_not(here))(away)


def most(ref):
    return ref.at[:, pl.ds(0, (HEADS - 1) * D)]


def each(count, step, carry):
    for j in range(count):
        carry = step(j, carry)
    return carry


def starts_in(len_ref):
    starts = [jnp.int32(0)]
    for i in range(DOCS - 1):
        starts.append(starts[-1] + len_ref[i])
    return starts


def start_of(pos, starts):
    best = jnp.zeros_like(pos)
    for s in starts[1:]:
        best = jnp.where(pos >= s, s, best)
    return best


def base_of(quarter, i):
    return pl.multiple_of((quarter + 4 * i) * BLOCK, BLOCK)


def rows8(row):
    return pl.ds(pl.multiple_of(row, 8), PIECE)


def back(taps, hit1, hit2, src, row, token):
    out = taps[0] * src[rows8(row), :]
    out = out + taps[1] * (src[pl.ds(row + 1, PIECE), :] * hit1[pl.ds(token + 1, PIECE), :])
    return out + taps[2] * (src[pl.ds(row + 2, PIECE), :] * hit2[pl.ds(token + 2, PIECE), :])


KEY, VALUE, QUERY, GRAD = range(4)


def kernel_body(
    q_ref, k_ref, v_ref, g_ref, all_taps, lengths, out,
    buf, xkv, ykv, xqg, xh, stage, spare, hit1, hit2, taps, size,
    kc, vc, kt, vt, qc, go, gt, sc, peak, whole, heads_out, dq, dk, dv,
    buf_a, buf_k, other, edge, got, corner,
    load, ssem, rsem, lsem, psem, tsem,
    ssem2, rsem2, lsem2, psem2, tsem2,
):
    me = Place()
    loads = [pltpu.make_async_copy(src, buf.at[n], load.at[n]) for n, src in enumerate((k_ref, v_ref, q_ref, g_ref))]
    for copy in loads:
        copy.start()
    few = [
        pltpu.make_async_copy(all_taps.at[:, :, columns(me.z)], taps, load.at[4]),
        pltpu.make_async_copy(lengths, size, load.at[5]),
    ]
    for copy in few:
        copy.start()

    barrier = pltpu.get_barrier_semaphore()
    signal(barrier, me.sibling())
    signal(barrier, me.quarter_at(1))
    for i in range(2):
        signal(barrier, me.leader(i))
    signal(barrier, me.token_at(0, 1)[1])
    pl.when(jnp.logical_not(me.home))(lambda: signal(barrier, me.token_at(0, 0)[1]))

    for i in range(1, OWN):
        for side in range(2):
            signal(barrier, me.token_at(i, side)[1])
    for copy in loads:
        copy.wait()
    greeted = 2 * HEADS + 2 - jnp.where(me.home, 1, 0) + jnp.where(me.last, HEADS, 0)
    pl.semaphore_wait(barrier, greeted)

    def send_kv(n, i, chip):
        head, device = me.owner_at(i, chip)
        side = jnp.where(me.yl == chip, 0, 1)
        remote(buf.at[n, :, columns(head)], xkv.at[n, side, me.slot], ssem.at[2 * n + chip], rsem.at[2 * n + side], device).start()

    def keep_kv(n):
        return pltpu.make_async_copy(buf.at[n, :, columns(me.head)], xkv.at[n, 0, me.slot], lsem.at[n])

    def send_qg(n, i):
        head, device = me.owner_at(i, me.yl)
        remote(buf.at[n, :, columns(head)], xqg.at[n - 2, me.slot], ssem.at[2 + n], rsem.at[2 + n], device).start()

    def keep_qg(n):
        return pltpu.make_async_copy(buf.at[n, :, columns(me.head)], xqg.at[n - 2, me.slot], lsem.at[n])

    for n in (QUERY, KEY, VALUE, GRAD):
        if n < 2:
            for chip in range(2):
                either(me.home & (me.yl == chip), lambda: keep_kv(n).start(), lambda: send_kv(n, 0, chip))

            for i in range(1, HEADS):
                send_kv(n, i, 0)
                send_kv(n, i, 1)
        else:
            either(me.home, lambda: keep_qg(n).start(), lambda: send_qg(n, 0))

            for i in range(1, HEADS):
                send_qg(n, i)
        if n == QUERY:
            @pl.when(me.last)
            def _():
                block = me.z // 2
                for i in range(HEADS):
                    head, device = me.follower_at(i)
                    remote(buf.at[QUERY, :, columns(head)], xh.at[block], ssem.at[6], tsem.at[block], device).start()

    swaps = [remote(xkv.at[n], ykv.at[n], psem.at[n], tsem.at[2 + n], me.sibling()) for n in range(2)]
    for copy in few:
        copy.wait()
    starts = starts_in(size)

    def hits(i, _):
        base = pl.multiple_of(i * 256, 256)
        pos = base + lax.broadcasted_iota(jnp.int32, (256, 1), 0)
        since = pos - start_of(pos, starts)
        hit1[pl.ds(base, 256), :] = jnp.broadcast_to(jnp.where(since >= 1, 1.0, 0.0).astype(F32), (256, D))
        hit2[pl.ds(base, 256), :] = jnp.broadcast_to(jnp.where(since >= 2, 1.0, 0.0).astype(F32), (256, D))
        return 0

    lax.fori_loop(0, T // 256, hits, 0)
    for ref in (hit1, hit2):
        ref[T:, :] = jnp.zeros((8, D), F32)
    for a in range(3):
        stage[a, 0:8, :] = jnp.zeros((8, D), F32)
    for ref in (dk, dv):
        ref[...] = jnp.zeros(ref.shape, F32)
    for i in range(2):
        dq[i, 0:PIECE, :] = jnp.zeros((PIECE, D), F32)
        dq[i, PIECE + BLOCK :, :] = jnp.zeros((8, D), F32)

    def unpack(n, ref, mine):
        def step(i, _):
            for side in range(2):
                base = base_of(me.quarter_of(mine, side), i)
                for j in range(PER_BLOCK):
                    stage[1 + n, rows8(base + j * PIECE + 8), :] = ref[n, side, i * PER_BLOCK + j].astype(F32)
            return 0

        lax.fori_loop(0, 2, step, 0)

    def mixed(a, base, rows):
        mix = taps[a, 0:1, :] * stage[a, pl.ds(base + 8, rows), :]
        mix = mix + taps[a, 1:2, :] * (stage[a, pl.ds(base + 7, rows), :] * hit1[pl.ds(base, rows), :])
        return mix + taps[a, 2:3, :] * (stage[a, pl.ds(base + 6, rows), :] * hit2[pl.ds(base, rows), :])

    def arrive_kv(n):
        settle(me.home, xkv.at[n, 0], xkv.at[n, 0, pl.ds(0, OWN - 1)], rsem.at[2 * n])
        drain(xkv.at[n, 1], rsem.at[2 * n + 1])
        pl.when(me.home)(lambda: keep_kv(n).wait())
        swaps[n].start()

    def convolve_kv(n, dst, dst_t):
        def mix_rows(base, rows):
            mix = mixed(1 + n, base, rows)
            dst[pl.ds(base, rows), :] = mix.astype(BF16)
            dst_t[:, pl.ds(base, rows)] = mix.T.astype(BF16)

        def blocks(is_own):
            def step(i, _):
                for side in range(2):
                    mix_rows(base_of(me.quarter_of(is_own, side), i), BLOCK)
                return 0

            lax.fori_loop(0, 2, step, 0)

        unpack(n, xkv, True)
        blocks(True)
        swaps[n].wait_recv()
        unpack(n, ykv, False)
        blocks(False)
        for i in range(2):
            mix_rows(base_of(me.core * 2, i), D)

    def arrive_qg(n):
        settle(me.home, xqg.at[n - 2], xqg.at[n - 2, pl.ds(0, OWN - 1)], rsem.at[2 + n])
        pl.when(me.home)(lambda: keep_qg(n).wait())

    arrive_qg(QUERY)
    before = lax.rem(me.quarter + 3, 4)
    for i in range(2):
        drain(xh.at[i], tsem.at[i])
        stage[0, rows8(base_of(before, i) + BLOCK - PIECE + 8), :] = xh[i].astype(F32)

    def unpack_q(i, _):
        base = base_of(me.quarter, i)
        for j in range(PER_BLOCK):
            stage[0, rows8(base + j * PIECE + 8), :] = xqg[0, i * PER_BLOCK + j].astype(F32)
        qc[i] = mixed(0, base, BLOCK).astype(BF16)
        return 0

    lax.fori_loop(0, 2, unpack_q, 0)
    arrive_kv(KEY)
    convolve_kv(KEY, kc, kt)

    def keys_of(i):
        t0 = base_of(me.quarter, i)
        from_row = jnp.maximum(t0 - LONGEST, 0) if i else 0
        return t0, from_row, TILES[i]

    def tile(from_row, j):
        return pl.multiple_of(from_row + j * BK, D) if not isinstance(from_row, int) else from_row + j * BK

    def scores(i):
        t0, from_row, tiles = keys_of(i)
        q = qc[i]
        tpos = t0 + lax.broadcasted_iota(jnp.int32, (1, BQ), 1)
        tstart = start_of(tpos, starts)
        uio = lax.broadcasted_iota(jnp.int32, (BK, BQ), 0)

        def score(j, m):
            u0 = tile(from_row, j)
            s = lax.dot_general(kc[pl.ds(u0, BK), :], q, NT, preferred_element_type=F32)
            s = jnp.where((uio <= tpos - u0) & (uio >= tstart - u0), s, MASKED)
            sc[i, pl.ds(u0, BK), :] = s
            return jnp.maximum(m, jnp.max(s, axis=0, keepdims=True))

        m = each(tiles, score, jnp.full((1, BQ), MASKED, F32))
        peak[i] = m * (SCALE * LOG2E)

    def forward(i, _):
        _, from_row, tiles = keys_of(i)
        shift = peak[i]

        def weigh(j, carry):
            total, o = carry
            u0 = tile(from_row, j)
            p = jnp.exp2(sc[i, pl.ds(u0, BK), :] * (SCALE * LOG2E) - shift)
            sc[i, pl.ds(u0, BK), :] = p
            total = total + jnp.sum(p, axis=0, keepdims=True)
            o = o + dot(vt[:, pl.ds(u0, BK)], p.astype(BF16))
            return total, o

        total, o = each(tiles, weigh, (jnp.zeros((1, BQ), F32), jnp.zeros((D, BQ), F32)))
        inv = 1.0 / total
        o = o * inv
        whole[i] = inv
        heads_out[i] = o
        spare[...] = o.T
        for j in range(PER_BLOCK):
            buf_a[0, i * PER_BLOCK + j] = spare[j * PIECE : (j + 1) * PIECE, :].astype(BF16)
        return 0

    scores(1)
    arrive_kv(VALUE)
    scores(0)
    convolve_kv(VALUE, vc, vt)
    for i in range(2):
        forward(i, 0)

    mine = columns(me.head)
    out_a, out_k = out.at[2], out.at[pl.ds(0, 2)]

    def send_a(n, i):
        s, device = me.token_at(i, 0)
        remote(buf_a.at[n, s], out_a.at[n, :, mine], ssem2.at[2 + n], rsem2.at[2 + n], device).start()

    def keep_a(n):
        return pltpu.make_async_copy(buf_a.at[n, me.slot], out_a.at[n, :, mine], lsem2.at[n])

    def send_k(i, side):
        s, device = me.token_at(i, side)
        remote(buf_k.at[side, s], out_k.at[side, :, :, mine], ssem2.at[side], rsem2.at[side], device).start()

    def keep_k():
        return pltpu.make_async_copy(buf_k.at[0, me.slot], out_k.at[0, :, :, mine], lsem2.at[2])

    either(me.home, lambda: keep_a(0).start(), lambda: send_a(0, 0))

    for i in range(1, OWN):
        send_a(0, i)
    arrive_qg(GRAD)

    def unpack_g(i, _):
        for j in range(PER_BLOCK):
            spare[j * PIECE : (j + 1) * PIECE, :] = xqg[1, i * PER_BLOCK + j].astype(F32)
        g = spare[...]
        go[i] = g.astype(BF16)
        gt[i] = g.T
        return 0

    lax.fori_loop(0, 2, unpack_g, 0)

    def gradients(i, _):
        _, from_row, tiles = keys_of(i)
        q, g, inv = qc[i], go[i], whole[i]
        delta = jnp.sum(gt[i] * heads_out[i], axis=0, keepdims=True)

        def grads(j, acc):
            u0 = tile(from_row, j)
            p = sc[i, pl.ds(u0, BK), :] * inv
            dp = lax.dot_general(vc[pl.ds(u0, BK), :], g, NT, preferred_element_type=F32)
            ds = (p * (dp - delta)).astype(BF16)
            dk[pl.ds(u0, BK), :] += dot(ds, q)
            dv[pl.ds(u0, BK), :] += dot(p.astype(BF16), g)
            return acc + dot(kt[:, pl.ds(u0, BK)], ds)

        acc = each(tiles, grads, jnp.zeros((D, BQ), F32))
        dq[i, PIECE : PIECE + BLOCK, :] = acc.T
        return 0

    for i in range(2):
        gradients(i, 0)
    scaled = [[taps[a, n : n + 1, :] * (SCALE if a < 2 else 1.0) for n in range(3)] for a in range(3)]

    def through(a, src, row, token):
        return back(scaled[a], hit1, hit2, src, row, token)

    def keys_at(quarter, i, j):
        token = base_of(quarter, i) + j * PIECE
        return through(1, dk, token, token), through(2, dv, token, token)

    def rest(i, _):
        for side in range(2):
            for j in range(PER_BLOCK):
                grad_k, grad_v = keys_at(me.quarter_of(False, side), i, j)
                other[side, i * PER_BLOCK + j, 0] = grad_k.astype(BF16)
                other[side, i * PER_BLOCK + j, 1] = grad_v.astype(BF16)
        token = base_of(before, i) + BLOCK - PIECE
        after = jnp.minimum(i + jnp.where(me.quarter == 0, 1, 0), 1)
        edge[i] = through(0, dq.at[after], 0, token).astype(BF16)
        return 0

    lax.fori_loop(0, 2, rest, 0)
    swap = remote(other, got, psem2.at[0], tsem2.at[0], me.sibling())
    turn = remote(edge, corner, psem2.at[1], tsem2.at[1], me.quarter_at(-1))
    swap.start()
    turn.start()

    def all_a(edges):
        for i in range(OWN):
            s, _ = me.token_at(i, 0)
            block, j = s // PER_BLOCK, lax.rem(s, PER_BLOCK)

            @pl.when((j == PER_BLOCK - 1) == edges)
            def _():
                grad = through(0, dq.at[block], (j + 1) * PIECE, base_of(me.quarter, block) + j * PIECE)
                if edges:
                    grad = grad + corner[block].astype(F32)
                buf_a[1, s] = grad.astype(BF16)
                if i:
                    send_a(1, i)
                else:
                    either(me.home, lambda: keep_a(1).start(), lambda: send_a(1, 0))

    all_a(False)
    turn.wait()
    all_a(True)
    swap.wait()

    def fill_k(i):
        s, _ = me.token_at(i, 0)
        for side in range(2):
            grads = keys_at(me.quarter_of(True, side), s // PER_BLOCK, lax.rem(s, PER_BLOCK))
            for n, grad in enumerate(grads):
                buf_k[side, s, n] = (grad + got[side, s, n].astype(F32)).astype(BF16)

    fill_k(0)
    either(me.home, lambda: keep_k().start(), lambda: send_k(0, 0))
    send_k(0, 1)

    for i in range(1, OWN):
        fill_k(i)
        send_k(i, 0)
        send_k(i, 1)

    for n in range(2):
        for chip in range(2):
            settle(me.home & (me.yl == chip), buf.at[n], most(buf.at[n]), ssem.at[2 * n + chip])
        settle(me.home, buf.at[2 + n], most(buf.at[2 + n]), ssem.at[4 + n])
        swaps[n].wait_send()
    pl.when(me.last)(lambda: drain(buf.at[QUERY], ssem.at[6]))
    for n in range(2):
        pl.when(me.home)(lambda: keep_a(n).wait())
        settle(me.home, out_a.at[n], most(out_a.at[n]), rsem2.at[2 + n])
        settle(me.home, buf_a.at[n], buf_a.at[n, pl.ds(0, OWN - 1)], ssem2.at[2 + n])
    pl.when(me.home)(lambda: keep_k().wait())
    settle(me.home, out_k.at[0], out_k.at[0, :, :, pl.ds(0, (HEADS - 1) * D)], rsem2.at[0])
    drain(out_k.at[1], rsem2.at[1])
    settle(me.home, buf_k.at[0], buf_k.at[0, pl.ds(0, OWN - 1)], ssem2.at[0])
    drain(buf_k.at[1], ssem2.at[1])


def everything(*arrays):
    hbm = pl.BlockSpec(memory_space=pltpu.HBM)
    pieces = functools.partial(pltpu.VMEM, dtype=BF16)
    dma = pltpu.SemaphoreType.DMA
    return pl.pallas_call(
        kernel_body,
        out_shape=pltpu.VMEM((3, 2, PIECE, HEADS * D), BF16),
        in_specs=[hbm] * 6,
        out_specs=pl.BlockSpec(memory_space=pl.ANY),
        scratch_shapes=[
            pieces((4, PIECE, HEADS * D)),
            pieces((2, 2, OWN, PIECE, D)), pieces((2, 2, OWN, PIECE, D)),
            pieces((2, OWN, PIECE, D)), pieces((2, PIECE, D)),
            pltpu.VMEM((3, T + 8, D), F32), pltpu.VMEM((BLOCK, D), F32),
            pltpu.VMEM((T + 8, D), F32), pltpu.VMEM((T + 8, D), F32),
            pltpu.VMEM((3, 3, D), F32), pltpu.SMEM((DOCS,), jnp.int32),
            pieces((T, D)), pieces((T, D)), pieces((D, T)), pieces((D, T)),
            pieces((2, BLOCK, D)), pieces((2, BLOCK, D)), pltpu.VMEM((2, D, BLOCK), F32),
            pltpu.VMEM((2, T, BQ), F32), pltpu.VMEM((2, 1, BQ), F32), pltpu.VMEM((2, 1, BQ), F32), pltpu.VMEM((2, D, BQ), F32),
            pltpu.VMEM((2, PIECE + BLOCK + 8, D), F32), pltpu.VMEM((T + 8, D), F32), pltpu.VMEM((T + 8, D), F32),
            pieces((2, OWN, PIECE, D)), pieces((2, OWN, 2, PIECE, D)),
            pieces((2, OWN, 2, PIECE, D)), pieces((2, PIECE, D)),
            pieces((2, OWN, 2, PIECE, D)), pieces((2, PIECE, D)),
            dma((6,)), dma((7,)), dma((6,)), dma((4,)), dma((2,)), dma((4,)),
            dma((4,)), dma((4,)), dma((3,)), dma((2,)), dma((2,)),
        ],
        compiler_params=pltpu.CompilerParams(collective_id=0, has_side_effects=True, vmem_limit_bytes=52 << 20),
        name="everything",
    )(*(pltpu.with_memory_space_constraint(x, pltpu.HBM) for x in arrays))


def on_device(query_in, key_in, value_in, grad_out, kernel, lengths):
    out = everything(query_in, key_in, value_in, grad_out, kernel, lengths)
    summed = (out[0].astype(F32) + out[1].astype(F32)).astype(BF16)
    return out[2, 0], out[2, 1], summed[0], summed[1]


def solution(mesh):
    fine = Mesh(mesh.devices.reshape(SIZES), NAMES)
    rows = P(NAMES, None)
    return jax.shard_map(
        on_device,
        mesh=fine,
        in_specs=(rows, rows, rows, rows, P(None, None, ("x", "yh")), P()),
        out_specs=(rows,) * 4,
        check_vma=False,
    )
```

```python
import functools

import jax
import jax.numpy as jnp
from jax import lax
from jax.experimental import pallas as pl
from jax.experimental.pallas import tpu as pltpu
from jax.sharding import Mesh
from jax.sharding import PartitionSpec as P

NAMES = ("z", "yl", "core", "x", "yh")
SIZES = (4, 2, 2, 4, 2)
D = 128
T = 3072
HEADS = 32
PIECE = 24
BLOCK = 384
PER_BLOCK = BLOCK // PIECE
OWN = 32
DOCS = 12
BQ = BLOCK
BK = 768
TILES = (2, 3)
LONGEST = 1920
MASKED = -1.0e30
SCALE = D**-0.5
MIX = 13
LOG2E = 1.4426950408889634
NT = (((1,), (1,)), ((), ()))
F32, BF16 = jnp.float32, jnp.bfloat16
MESH = pl.DeviceIdType.MESH


def dot(a, b):
    return jnp.dot(a, b, preferred_element_type=F32)


class Place:
    def __init__(self):
        self.z, self.yl, self.core, self.x, self.yh = (lax.axis_index(n) for n in NAMES)
        self.takes = lax.rem(self.z, 2)
        self.head = (self.x * 2 + self.yh) * 4 + self.z
        self.slot = self.z // 2 * PER_BLOCK + self.core * 8 + self.x * 2 + self.yh
        self.home = self.core == self.takes
        self.quarter = self.core * 2 + self.yl
        self.last = (self.core == 1) & (self.x == 3) & (self.yh == 1)

    def owner_at(self, i, chip):
        i = i * MIX % 32
        z, yh, x = lax.rem(self.z + i % 4, 4), lax.rem(self.yh + i // 4 % 2, 2), lax.rem(self.x + i // 8, 4)
        return (x * 2 + yh) * 4 + z, dict(z=z, yl=chip, core=self.takes, x=x, yh=yh)

    def token_at(self, i, side):
        i = i * MIX % 32
        half, core = lax.rem(self.z // 2 + i // 16, 2), lax.rem(self.core + i // 8 % 2, 2)
        x, yh = lax.rem(self.x + i // 2 % 4, 4), lax.rem(self.yh + i % 2, 2)
        device = dict(z=half * 2 + self.core, yl=lax.rem(self.yl + side, 2), core=core, x=x, yh=yh)
        return ((half * 2 + core) * 4 + x) * 2 + yh, device

    def quarter_of(self, mine, side):
        return jnp.where(mine, self.core, 1 - self.core) * 2 + lax.rem(self.yl + side, 2)

    def other(self, yl, core):
        return dict(z=self.z, yl=yl, core=core, x=self.x, yh=self.yh)

    def sibling(self):
        return self.other(self.yl, 1 - self.core)

    def quarter_at(self, step):
        q = lax.rem(self.quarter + step + 4, 4)
        return self.other(lax.rem(q, 2), q // 2)

    def follower_at(self, i):
        k, device = self.owner_at(i, 0)
        q = lax.rem(self.takes * 2 + self.yl + 1, 4)
        return k, {**device, "yl": lax.rem(q, 2), "core": q // 2}

    def leader(self, i):
        q = lax.rem(self.quarter + 3, 4)
        return dict(z=q // 2 + 2 * i, yl=lax.rem(q, 2), core=1, x=3, yh=1)


def signal(sem, device):
    pl.semaphore_signal(sem, 1, device_id=device, device_id_type=MESH)


def remote(src, dst, send, recv, device):
    return pltpu.make_async_remote_copy(src, dst, send, recv, device_id=device, device_id_type=MESH)


def drain(ref, sem):
    pltpu.make_async_copy(ref, ref, sem).wait()


def columns(head):
    return pl.ds(pl.multiple_of(head * D, D), D)


def settle(fewer, ref, part, sem):
    @pl.when(fewer)
    def _():
        drain(part, sem)

    @pl.when(jnp.logical_not(fewer))
    def _():
        drain(ref, sem)


def either(here, local, away):
    pl.when(here)(local)
    pl.when(jnp.logical_not(here))(away)


def most(ref):
    return ref.at[:, pl.ds(0, (HEADS - 1) * D)]


def each(count, step, carry):
    for j in range(count):
        carry = step(j, carry)
    return carry


def starts_in(len_ref):
    starts = [jnp.int32(0)]
    for i in range(DOCS - 1):
        starts.append(starts[-1] + len_ref[i])
    return starts


def start_of(pos, starts):
    best = jnp.zeros_like(pos)
    for s in starts[1:]:
        best = jnp.where(pos >= s, s, best)
    return best


def base_of(quarter, i):
    return pl.multiple_of((quarter + 4 * i) * BLOCK, BLOCK)


def rows8(row):
    return pl.ds(pl.multiple_of(row, 8), PIECE)


def back(taps, hit1, hit2, src, row, token):
    out = taps[0] * src[rows8(row), :]
    out = out + taps[1] * (src[pl.ds(row + 1, PIECE), :] * hit1[pl.ds(token + 1, PIECE), :])
    return out + taps[2] * (src[pl.ds(row + 2, PIECE), :] * hit2[pl.ds(token + 2, PIECE), :])


KEY, VALUE, QUERY, GRAD = range(4)


def kernel_body(
    q_ref, k_ref, v_ref, g_ref, all_taps, lengths, out,
    buf, xkv, ykv, xqg, xh, stage, spare, hit1, hit2, taps, size,
    kc, vc, kt, vt, qc, go, gt, sc, peak, whole, heads_out, dq, dk, dv,
    buf_a, buf_k, other, edge, got, corner,
    load, ssem, rsem, lsem, psem, tsem,
    ssem2, rsem2, lsem2, psem2, tsem2,
):
    me = Place()
    loads = [pltpu.make_async_copy(src, buf.at[n], load.at[n]) for n, src in enumerate((k_ref, v_ref, q_ref, g_ref))]
    for copy in loads:
        copy.start()
    few = [
        pltpu.make_async_copy(all_taps.at[:, :, columns(me.z)], taps, load.at[4]),
        pltpu.make_async_copy(lengths, size, load.at[5]),
    ]
    for copy in few:
        copy.start()

    barrier = pltpu.get_barrier_semaphore()
    signal(barrier, me.sibling())
    signal(barrier, me.quarter_at(1))
    for i in range(2):
        signal(barrier, me.leader(i))
    signal(barrier, me.token_at(0, 1)[1])
    pl.when(jnp.logical_not(me.home))(lambda: signal(barrier, me.token_at(0, 0)[1]))

    for i in range(1, OWN):
        for side in range(2):
            signal(barrier, me.token_at(i, side)[1])
    for copy in loads:
        copy.wait()
    greeted = 2 * HEADS + 2 - jnp.where(me.home, 1, 0) + jnp.where(me.last, HEADS, 0)
    pl.semaphore_wait(barrier, greeted)

    def send_kv(n, i, chip):
        head, device = me.owner_at(i, chip)
        side = jnp.where(me.yl == chip, 0, 1)
        remote(buf.at[n, :, columns(head)], xkv.at[n, side, me.slot], ssem.at[2 * n + chip], rsem.at[2 * n + side], device).start()

    def keep_kv(n):
        return pltpu.make_async_copy(buf.at[n, :, columns(me.head)], xkv.at[n, 0, me.slot], lsem.at[n])

    def send_qg(n, i):
        head, device = me.owner_at(i, me.yl)
        remote(buf.at[n, :, columns(head)], xqg.at[n - 2, me.slot], ssem.at[2 + n], rsem.at[2 + n], device).start()

    def keep_qg(n):
        return pltpu.make_async_copy(buf.at[n, :, columns(me.head)], xqg.at[n - 2, me.slot], lsem.at[n])

    for n in (QUERY, KEY, VALUE, GRAD):
        if n < 2:
            for chip in range(2):
                either(me.home & (me.yl == chip), lambda: keep_kv(n).start(), lambda: send_kv(n, 0, chip))

            for i in range(1, HEADS):
                send_kv(n, i, 0)
                send_kv(n, i, 1)
        else:
            either(me.home, lambda: keep_qg(n).start(), lambda: send_qg(n, 0))

            for i in range(1, HEADS):
                send_qg(n, i)
        if n == QUERY:
            @pl.when(me.last)
            def _():
                block = me.z // 2
                for i in range(HEADS):
                    head, device = me.follower_at(i)
                    remote(buf.at[QUERY, :, columns(head)], xh.at[block], ssem.at[6], tsem.at[block], device).start()

    swaps = [remote(xkv.at[n], ykv.at[n], psem.at[n], tsem.at[2 + n], me.sibling()) for n in range(2)]
    for copy in few:
        copy.wait()
    starts = starts_in(size)

    def hits(i, _):
        base = pl.multiple_of(i * 256, 256)
        pos = base + lax.broadcasted_iota(jnp.int32, (256, 1), 0)
        since = pos - start_of(pos, starts)
        hit1[pl.ds(base, 256), :] = jnp.broadcast_to(jnp.where(since >= 1, 1.0, 0.0).astype(F32), (256, D))
        hit2[pl.ds(base, 256), :] = jnp.broadcast_to(jnp.where(since >= 2, 1.0, 0.0).astype(F32), (256, D))
        return 0

    lax.fori_loop(0, T // 256, hits, 0)
    for ref in (hit1, hit2):
        ref[T:, :] = jnp.zeros((8, D), F32)
    for a in range(3):
        stage[a, 0:8, :] = jnp.zeros((8, D), F32)
    for ref in (dk, dv):
        ref[...] = jnp.zeros(ref.shape, F32)
    for i in range(2):
        dq[i, 0:PIECE, :] = jnp.zeros((PIECE, D), F32)
        dq[i, PIECE + BLOCK :, :] = jnp.zeros((8, D), F32)

    def unpack(n, ref, mine):
        def step(i, _):
            for side in range(2):
                base = base_of(me.quarter_of(mine, side), i)
                for j in range(PER_BLOCK):
                    stage[1 + n, rows8(base + j * PIECE + 8), :] = ref[n, side, i * PER_BLOCK + j].astype(F32)
            return 0

        lax.fori_loop(0, 2, step, 0)

    def mixed(a, base, rows):
        mix = taps[a, 0:1, :] * stage[a, pl.ds(base + 8, rows), :]
        mix = mix + taps[a, 1:2, :] * (stage[a, pl.ds(base + 7, rows), :] * hit1[pl.ds(base, rows), :])
        return mix + taps[a, 2:3, :] * (stage[a, pl.ds(base + 6, rows), :] * hit2[pl.ds(base, rows), :])

    def arrive_kv(n):
        settle(me.home, xkv.at[n, 0], xkv.at[n, 0, pl.ds(0, OWN - 1)], rsem.at[2 * n])
        drain(xkv.at[n, 1], rsem.at[2 * n + 1])
        pl.when(me.home)(lambda: keep_kv(n).wait())
        swaps[n].start()

    def convolve_kv(n, dst, dst_t):
        def mix_rows(base, rows):
            mix = mixed(1 + n, base, rows)
            dst[pl.ds(base, rows), :] = mix.astype(BF16)
            dst_t[:, pl.ds(base, rows)] = mix.T.astype(BF16)

        def blocks(is_own):
            def step(i, _):
                for side in range(2):
                    mix_rows(base_of(me.quarter_of(is_own, side), i), BLOCK)
                return 0

            lax.fori_loop(0, 2, step, 0)

        unpack(n, xkv, True)
        blocks(True)
        swaps[n].wait_recv()
        unpack(n, ykv, False)
        blocks(False)
        for i in range(2):
            mix_rows(base_of(me.core * 2, i), D)

    def arrive_qg(n):
        settle(me.home, xqg.at[n - 2], xqg.at[n - 2, pl.ds(0, OWN - 1)], rsem.at[2 + n])
        pl.when(me.home)(lambda: keep_qg(n).wait())

    arrive_qg(QUERY)
    before = lax.rem(me.quarter + 3, 4)
    for i in range(2):
        drain(xh.at[i], tsem.at[i])
        stage[0, rows8(base_of(before, i) + BLOCK - PIECE + 8), :] = xh[i].astype(F32)

    def unpack_q(i, _):
        base = base_of(me.quarter, i)
        for j in range(PER_BLOCK):
            stage[0, rows8(base + j * PIECE + 8), :] = xqg[0, i * PER_BLOCK + j].astype(F32)
        qc[i] = mixed(0, base, BLOCK).astype(BF16)
        return 0

    lax.fori_loop(0, 2, unpack_q, 0)
    arrive_kv(KEY)
    convolve_kv(KEY, kc, kt)

    def keys_of(i):
        t0 = base_of(me.quarter, i)
        from_row = jnp.maximum(t0 - LONGEST, 0) if i else 0
        return t0, from_row, TILES[i]

    def tile(from_row, j):
        return pl.multiple_of(from_row + j * BK, D) if not isinstance(from_row, int) else from_row + j * BK

    def scores(i):
        t0, from_row, tiles = keys_of(i)
        q = qc[i]
        tpos = t0 + lax.broadcasted_iota(jnp.int32, (1, BQ), 1)
        tstart = start_of(tpos, starts)
        uio = lax.broadcasted_iota(jnp.int32, (BK, BQ), 0)

        def score(j, m):
            u0 = tile(from_row, j)
            s = lax.dot_general(kc[pl.ds(u0, BK), :], q, NT, preferred_element_type=F32)
            ok = uio >= tstart - u0
            if i == 0 or j == tiles - 1:
                ok = ok & (uio <= tpos - u0)
            s = jnp.where(ok, s, MASKED)
            sc[i, pl.ds(u0, BK), :] = s
            return jnp.maximum(m, jnp.max(s, axis=0, keepdims=True))

        m = each(tiles, score, jnp.full((1, BQ), MASKED, F32))
        peak[i] = m * (SCALE * LOG2E)

    def forward(i, _):
        _, from_row, tiles = keys_of(i)
        shift = peak[i]

        def weigh(j, carry):
            total, o = carry
            u0 = tile(from_row, j)
            p = jnp.exp2(sc[i, pl.ds(u0, BK), :] * (SCALE * LOG2E) - shift)
            sc[i, pl.ds(u0, BK), :] = p
            total = total + jnp.sum(p, axis=0, keepdims=True)
            o = o + dot(vt[:, pl.ds(u0, BK)], p.astype(BF16))
            return total, o

        total, o = each(tiles, weigh, (jnp.zeros((1, BQ), F32), jnp.zeros((D, BQ), F32)))
        inv = 1.0 / total
        o = o * inv
        whole[i] = inv
        heads_out[i] = o
        spare[...] = o.T
        for j in range(PER_BLOCK):
            buf_a[0, i * PER_BLOCK + j] = spare[j * PIECE : (j + 1) * PIECE, :].astype(BF16)
        return 0

    scores(1)
    arrive_kv(VALUE)
    scores(0)
    convolve_kv(VALUE, vc, vt)
    for i in range(2):
        forward(i, 0)

    mine = columns(me.head)
    out_a, out_k = out.at[2], out.at[pl.ds(0, 2)]

    def send_a(n, i):
        s, device = me.token_at(i, 0)
        remote(buf_a.at[n, s], out_a.at[n, :, mine], ssem2.at[2 + n], rsem2.at[2 + n], device).start()

    def keep_a(n):
        return pltpu.make_async_copy(buf_a.at[n, me.slot], out_a.at[n, :, mine], lsem2.at[n])

    def send_k(i, side):
        s, device = me.token_at(i, side)
        remote(buf_k.at[side, s], out_k.at[side, :, :, mine], ssem2.at[side], rsem2.at[side], device).start()

    def keep_k():
        return pltpu.make_async_copy(buf_k.at[0, me.slot], out_k.at[0, :, :, mine], lsem2.at[2])

    either(me.home, lambda: keep_a(0).start(), lambda: send_a(0, 0))

    for i in range(1, OWN):
        send_a(0, i)
    arrive_qg(GRAD)

    def unpack_g(i, _):
        for j in range(PER_BLOCK):
            spare[j * PIECE : (j + 1) * PIECE, :] = xqg[1, i * PER_BLOCK + j].astype(F32)
        g = spare[...]
        go[i] = g.astype(BF16)
        gt[i] = g.T
        return 0

    lax.fori_loop(0, 2, unpack_g, 0)

    def gradients(i, _):
        _, from_row, tiles = keys_of(i)
        q, g, inv = qc[i], go[i], whole[i]
        delta = jnp.sum(gt[i] * heads_out[i], axis=0, keepdims=True)

        def grads(j, acc):
            u0 = tile(from_row, j)
            p = sc[i, pl.ds(u0, BK), :] * inv
            dp = lax.dot_general(vc[pl.ds(u0, BK), :], g, NT, preferred_element_type=F32)
            ds = (p * (dp - delta)).astype(BF16)
            dk[pl.ds(u0, BK), :] += dot(ds, q)
            dv[pl.ds(u0, BK), :] += dot(p.astype(BF16), g)
            return acc + dot(kt[:, pl.ds(u0, BK)], ds)

        acc = each(tiles, grads, jnp.zeros((D, BQ), F32))
        dq[i, PIECE : PIECE + BLOCK, :] = acc.T
        return 0

    for i in range(2):
        gradients(i, 0)
    scaled = [[taps[a, n : n + 1, :] * (SCALE if a < 2 else 1.0) for n in range(3)] for a in range(3)]

    def through(a, src, row, token):
        return back(scaled[a], hit1, hit2, src, row, token)

    def keys_at(quarter, i, j):
        token = base_of(quarter, i) + j * PIECE
        return through(1, dk, token, token), through(2, dv, token, token)

    def rest(i, _):
        for side in range(2):
            for j in range(PER_BLOCK):
                grad_k, grad_v = keys_at(me.quarter_of(False, side), i, j)
                other[side, i * PER_BLOCK + j, 0] = grad_k.astype(BF16)
                other[side, i * PER_BLOCK + j, 1] = grad_v.astype(BF16)
        token = base_of(before, i) + BLOCK - PIECE
        after = jnp.minimum(i + jnp.where(me.quarter == 0, 1, 0), 1)
        edge[i] = through(0, dq.at[after], 0, token).astype(BF16)
        return 0

    lax.fori_loop(0, 2, rest, 0)
    swap = remote(other, got, psem2.at[0], tsem2.at[0], me.sibling())
    turn = remote(edge, corner, psem2.at[1], tsem2.at[1], me.quarter_at(-1))
    swap.start()
    turn.start()

    def all_a(edges):
        for i in range(OWN):
            s, _ = me.token_at(i, 0)
            block, j = s // PER_BLOCK, lax.rem(s, PER_BLOCK)

            @pl.when((j == PER_BLOCK - 1) == edges)
            def _():
                grad = through(0, dq.at[block], (j + 1) * PIECE, base_of(me.quarter, block) + j * PIECE)
                if edges:
                    grad = grad + corner[block].astype(F32)
                buf_a[1, s] = grad.astype(BF16)
                if i:
                    send_a(1, i)
                else:
                    either(me.home, lambda: keep_a(1).start(), lambda: send_a(1, 0))

    all_a(False)
    turn.wait()
    all_a(True)
    swap.wait()

    def fill_k(i):
        s, _ = me.token_at(i, 0)
        for side in range(2):
            grads = keys_at(me.quarter_of(True, side), s // PER_BLOCK, lax.rem(s, PER_BLOCK))
            for n, grad in enumerate(grads):
                buf_k[side, s, n] = (grad + got[side, s, n].astype(F32)).astype(BF16)

    fill_k(0)
    either(me.home, lambda: keep_k().start(), lambda: send_k(0, 0))
    send_k(0, 1)

    for i in range(1, OWN):
        fill_k(i)
        send_k(i, 0)
        send_k(i, 1)

    for n in range(2):
        for chip in range(2):
            settle(me.home & (me.yl == chip), buf.at[n], most(buf.at[n]), ssem.at[2 * n + chip])
        settle(me.home, buf.at[2 + n], most(buf.at[2 + n]), ssem.at[4 + n])
        swaps[n].wait_send()
    pl.when(me.last)(lambda: drain(buf.at[QUERY], ssem.at[6]))
    for n in range(2):
        pl.when(me.home)(lambda: keep_a(n).wait())
        settle(me.home, out_a.at[n], most(out_a.at[n]), rsem2.at[2 + n])
        settle(me.home, buf_a.at[n], buf_a.at[n, pl.ds(0, OWN - 1)], ssem2.at[2 + n])
    pl.when(me.home)(lambda: keep_k().wait())
    settle(me.home, out_k.at[0], out_k.at[0, :, :, pl.ds(0, (HEADS - 1) * D)], rsem2.at[0])
    drain(out_k.at[1], rsem2.at[1])
    settle(me.home, buf_k.at[0], buf_k.at[0, pl.ds(0, OWN - 1)], ssem2.at[0])
    drain(buf_k.at[1], ssem2.at[1])


def everything(*arrays):
    hbm = pl.BlockSpec(memory_space=pltpu.HBM)
    pieces = functools.partial(pltpu.VMEM, dtype=BF16)
    dma = pltpu.SemaphoreType.DMA
    return pl.pallas_call(
        kernel_body,
        out_shape=pltpu.VMEM((3, 2, PIECE, HEADS * D), BF16),
        in_specs=[hbm] * 6,
        out_specs=pl.BlockSpec(memory_space=pl.ANY),
        scratch_shapes=[
            pieces((4, PIECE, HEADS * D)),
            pieces((2, 2, OWN, PIECE, D)), pieces((2, 2, OWN, PIECE, D)),
            pieces((2, OWN, PIECE, D)), pieces((2, PIECE, D)),
            pltpu.VMEM((3, T + 8, D), F32), pltpu.VMEM((BLOCK, D), F32),
            pltpu.VMEM((T + 8, D), F32), pltpu.VMEM((T + 8, D), F32),
            pltpu.VMEM((3, 3, D), F32), pltpu.SMEM((DOCS,), jnp.int32),
            pieces((T, D)), pieces((T, D)), pieces((D, T)), pieces((D, T)),
            pieces((2, BLOCK, D)), pieces((2, BLOCK, D)), pltpu.VMEM((2, D, BLOCK), F32),
            pltpu.VMEM((2, T, BQ), F32), pltpu.VMEM((2, 1, BQ), F32), pltpu.VMEM((2, 1, BQ), F32), pltpu.VMEM((2, D, BQ), F32),
            pltpu.VMEM((2, PIECE + BLOCK + 8, D), F32), pltpu.VMEM((T + 8, D), F32), pltpu.VMEM((T + 8, D), F32),
            pieces((2, OWN, PIECE, D)), pieces((2, OWN, 2, PIECE, D)),
            pieces((2, OWN, 2, PIECE, D)), pieces((2, PIECE, D)),
            pieces((2, OWN, 2, PIECE, D)), pieces((2, PIECE, D)),
            dma((6,)), dma((7,)), dma((6,)), dma((4,)), dma((2,)), dma((4,)),
            dma((4,)), dma((4,)), dma((3,)), dma((2,)), dma((2,)),
        ],
        compiler_params=pltpu.CompilerParams(collective_id=0, has_side_effects=True, vmem_limit_bytes=52 << 20),
        name="everything",
    )(*(pltpu.with_memory_space_constraint(x, pltpu.HBM) for x in arrays))


def on_device(query_in, key_in, value_in, grad_out, kernel, lengths):
    out = everything(query_in, key_in, value_in, grad_out, kernel, lengths)
    summed = (out[0].astype(F32) + out[1].astype(F32)).astype(BF16)
    return out[2, 0], out[2, 1], summed[0], summed[1]


def solution(mesh):
    fine = Mesh(mesh.devices.reshape(SIZES), NAMES)
    rows = P(NAMES, None)
    return jax.shard_map(
        on_device,
        mesh=fine,
        in_specs=(rows, rows, rows, rows, P(None, None, ("x", "yh")), P()),
        out_specs=(rows,) * 4,
        check_vma=False,
    )
```
